256 devices in a mesh: grp: 8 (over y, core), col: 32 (over x, z).
Axes of the slice: x: 4, y: 4, z: 8, core: 2. Of those that a mesh axis runs over, the one named last changes fastest.
Arguments:
- tiles: float32 [8, 32, 192, 128, 128], P('grp', 'col')
- tile_rows: int32 [8, 32, 192], P('grp', 'col'), may hold values from 0 to 31
- tile_cols: int32 [8, 32, 192], P('grp', 'col'), may hold values from 0 to 3
- bucket_fill: int32 [8, 32, 32], P('grp', 'col'), may hold values from 1 to 6, as said below
- row_slot: int32 [8, 32], P('grp'), may hold values from 0 to 31, each once within a row
- sketch: float32 [16384, 256], P('col'), may hold values from -6 to 6
Outputs:
- embedding: float32 [32768, 256], P(('grp', 'col'))
- factor: float32 [256, 256], replicated
The draws below stay inside these ranges and needn't reach their ends.
Inputs may be any that keep to these rules, and one draw needn't show every extreme that they name: `bucket_fill`: every device has at least one bucket with all 6 slots live.
All inputs are finite; a program needn't handle non-finite values.
Results may differ from the reference program's by a relative error of at most 0.0003.
Values sent between devices are 32-bit elements; how exact they have to be, the bound alone decides.
No kernel may reach another device: no remote copies, remote signals or barrier semaphores. Data moves between devices by JAX's collectives and lax.ppermute only.
A program may use at most 192 MiB of HBM per device.

```python
import math
import jax
import jax.numpy as jnp
import numpy as np
from jax import lax

TILE = 128
K = 256
CB_DEV = 4
CAP = 6
GROUPS = 8
SHARDS = 32
SLOTS = 192
RB_GRP = 32
ROWS = 32768
COLS = 16384


def draw_tiles(key, part):
    key = jax.random.fold_in(key, 11)
    first_key, second_key = jax.random.split(key)
    shape = (GROUPS, SHARDS, SLOTS, TILE, TILE)
    base = jax.random.normal(first_key, shape, jnp.float32)
    spread = math.log(4.0)
    row_scale = jnp.exp(jax.random.uniform(second_key, (GROUPS, SHARDS, SLOTS, TILE, 1), jnp.float32, 0.0, spread))
    device = (jnp.arange(GROUPS)[:, None] * SHARDS + jnp.arange(SHARDS)[None, :]).astype(jnp.float32)
    rising = 1.0 + 2.0 * device / max(GROUPS * SHARDS - 1, 1)
    return base * row_scale * rising[:, :, None, None, None] / math.sqrt(TILE)


def draw_bucket_fill(key, part):
    key = jax.random.fold_in(key, 23)
    first_key, second_key = jax.random.split(key)
    counts = jax.random.randint(first_key, (GROUPS, SHARDS, SHARDS), 1, CAP + 1)
    position = jax.random.randint(second_key, (GROUPS, SHARDS, 1), 0, SHARDS)
    bucket_ids = jnp.arange(SHARDS)[None, None, :]
    return jnp.where(bucket_ids == position, CAP, counts).astype(jnp.int32)


def place_ends(entries, rng, least, largest):
    longest = entries.shape.index(max(entries.shape))
    spots = []
    for shift in (0, 1):
        where = [jax.random.randint(jax.random.fold_in(rng, axis), (), 0, length) for axis, length in enumerate(entries.shape)]
        where[longest] = (where[longest] + shift) % entries.shape[longest]
        spots.append(tuple(where))
    return entries.at[spots[0]].set(least).at[spots[1]].set(largest)


def steps_of(rng, shape, cuts, smallest, top_value):
    def one(dim, parts):
        draws = jax.random.uniform(jax.random.fold_in(jax.random.fold_in(rng, 6), dim), (parts,), jnp.float32, smallest / len(cuts), top_value / len(cuts))
        return jnp.repeat(jnp.exp(draws), shape[dim] // parts).reshape((-1,) + (1,) * (len(shape) - dim - 1))

    gain = one(*cuts[0])
    for cut in cuts[1:]:
        gain = gain * one(*cut)
    return gain


def cumulative_ranks(count, slope):
    portions = [(1 << 20) // math.isqrt(rank ** slope) + 1 for rank in range(1, count + 1)]
    deviation = 1 + sum(portions) // (1 << 30)
    return np.cumsum(np.array([max(1, weight // deviation) for weight in portions]))


def skewed_ids(stream_key, dims, count, lean):
    grid = cumulative_ranks(count, lean)
    pick = jax.random.randint(jax.random.fold_in(stream_key, 1), dims, 0, int(grid[count - 1]))
    grade = jnp.searchsorted(jnp.asarray(grid, jnp.int32), pick, side="right")
    return jax.random.permutation(jax.random.fold_in(stream_key, 2), count)[grade].astype(jnp.int32)


def scatter_about(key, dims, deviation, most, cuts=(), held_as=jnp.bfloat16):
    entries = jax.random.normal(key, dims, jnp.float32) * deviation
    if len(cuts) > 0:
        entries = steps_of(key, dims, cuts, -0.22, 0.18) * entries
    return jnp.clip(entries, min=-most, max=most).astype(held_as)


def setup_inputs(seed: int = 0) -> dict:
    seeds = jax.random.split(jax.random.key(seed), 7)
    tiles = draw_tiles(jax.random.fold_in(seeds[6], 71), 0)
    tile_rows = place_ends(jax.random.randint(seeds[1], (GROUPS, SHARDS, SLOTS), 0, RB_GRP), jax.random.fold_in(seeds[1], 1), 0, RB_GRP - 1).astype(jnp.int32)
    tile_cols = place_ends(skewed_ids(seeds[2], (GROUPS, SHARDS, SLOTS), CB_DEV, 2), jax.random.fold_in(seeds[2], 3), 0, CB_DEV - 1).astype(jnp.int32)
    bucket_fill = draw_bucket_fill(jax.random.fold_in(seeds[6], 71), 0)
    row_slot = jax.vmap(lambda own: jax.random.permutation(own, RB_GRP))(jax.random.split(seeds[4], GROUPS)).reshape((GROUPS, RB_GRP)).astype(jnp.int32)
    sketch = scatter_about(seeds[5], (COLS, K), 1.0, 6.0, ((0, 32),), jnp.float32)
    return dict(tiles=tiles, tile_rows=tile_rows, tile_cols=tile_cols, bucket_fill=bucket_fill, row_slot=row_slot, sketch=sketch)


def reference(tiles, tile_rows, tile_cols, bucket_fill, row_slot, sketch):
    sketch_blocks = sketch.reshape(COLS // TILE, TILE, K)
    slot_ids = jnp.arange(SLOTS, dtype=jnp.int32)
    bucket_of = slot_ids // CAP
    block_ids = jnp.arange(RB_GRP, dtype=jnp.int32)

    def one_group(packed):
        tiles_g, rows_g, cols_g, fill_g, slot_g = packed

        def add_device(running, device):
            tiles_d, rows_d, cols_d, fill_d = device
            live_flag = slot_ids % CAP < fill_d[bucket_of]
            column_block = (bucket_of * CB_DEV + cols_d).astype(jnp.int32)
            panels = sketch_blocks[column_block]
            products = jnp.einsum('tij,tjk->tik', tiles_d, panels, precision=lax.Precision.HIGHEST)
            target = slot_g[rows_d]
            selector = ((target[None, :] == block_ids[:, None]) & live_flag[None, :]).astype(jnp.float32)
            added = jnp.einsum('st,tik->sik', selector, products, precision=lax.Precision.HIGHEST)
            return (running + added, 0)
        start_sum = jnp.zeros((RB_GRP, TILE, K), jnp.float32)
        running, unused = lax.scan(add_device, start_sum, (tiles_g, rows_g, cols_g, fill_g))
        return running
    slabs = lax.map(one_group, (tiles, tile_rows, tile_cols, bucket_fill, row_slot))
    product_rows = slabs.reshape(ROWS, K)
    gram_matrix = jnp.dot(product_rows.T.astype(jnp.float32), product_rows.astype(jnp.float32), precision=lax.Precision.HIGHEST, preferred_element_type=jnp.float32)
    lower_factor = jnp.linalg.cholesky(gram_matrix)
    row_scale = jnp.sqrt(jnp.float32(ROWS))
    solved = lax.linalg.triangular_solve(lower_factor, product_rows, left_side=False, lower=True, transpose_a=True)
    embedding = solved * row_scale
    factor = lower_factor.T / row_scale
    return (embedding, factor)
```

```python
import jax
import jax.numpy as jnp
from jax import lax
from jax.experimental import pallas as pl
from jax.experimental.pallas import tpu as pltpu
from jax.sharding import Mesh
from jax.sharding import PartitionSpec as P

AXES = ("y", "core", "x", "z")
SIZES = (4, 2, 4, 8)
EDGE = 128
WIDTH = 256
BLOCKS = 32
BUCKETS = 32
PER_BUCKET = 6
SLOTS = 192
ROWS = 32768
GROUP = 4


def shift(value, axis, step):
    count = lax.axis_size(axis)
    return lax.ppermute(value, axis, [(i, (i + step) % count) for i in range(count)])


def ring_gather(block, axis):
    count = lax.axis_size(axis)
    found = [None] * count
    found[0] = (block,)
    behind = ahead = block
    for step in range(1, count // 2):
        behind = shift(behind, axis, 1)
        ahead = shift(ahead, axis, -1)
        found[count - step] = (behind,)
        found[step] = (ahead,)
    half = block.shape[0] // 2
    found[count // 2] = (shift(behind[:half], axis, 1), shift(ahead[half:], axis, -1))
    return found


def products_kernel(fill, blk, row, *refs):
    tiles = refs[0]
    pieces = refs[1:15]
    outs = refs[15:20]
    panels, held, total, order, tile_sem, piece_sem, out_sem = refs[20:]

    offset = 0
    piece_copies = []
    for n, piece in enumerate(pieces):
        length = piece.shape[0]
        copy = pltpu.make_async_copy(piece, panels.at[pl.ds(offset, length)], piece_sem.at[n])
        copy.start()
        piece_copies.append(copy)
        offset += length

    def tile_copy(b):
        span = pl.ds(b * PER_BUCKET, PER_BUCKET)
        return pltpu.make_async_copy(tiles.at[span], held.at[span], tile_sem.at[b])

    @pl.loop(0, BUCKETS)
    def _(b):
        tile_copy(b).start()

    def list_bucket(b, count):
        def put(j, c):
            order[c] = b * PER_BUCKET + j
            return c + 1

        return lax.fori_loop(0, fill[b], put, count)

    total[...] = jnp.zeros_like(total)

    def product(slot):
        tile = held[slot]
        panel = panels[pl.ds(pl.multiple_of(blk[slot] * EDGE, EDGE), EDGE), :]
        tile_hi = tile.astype(jnp.bfloat16)
        tile_lo = (tile - tile_hi.astype(jnp.float32)).astype(jnp.bfloat16)
        panel_hi = panel.astype(jnp.bfloat16)
        panel_lo = (panel - panel_hi.astype(jnp.float32)).astype(jnp.bfloat16)
        left = jnp.concatenate([tile_hi, tile_hi, tile_lo], axis=1)
        right = jnp.concatenate([panel_hi, panel_lo, panel_hi], axis=0)
        return jnp.dot(left, right, preferred_element_type=jnp.float32)

    for copy in piece_copies:
        copy.wait()

    def quarter(q, start):
        first = q * (BUCKETS // 4)

        @pl.loop(first, first + BUCKETS // 4)
        def _(b):
            tile_copy(b).wait()

        stop = lax.fori_loop(first, first + BUCKETS // 4, list_bucket, start)
        groups = (stop - start) // GROUP

        @pl.loop(0, groups)
        def _(g):
            slots = [order[start + g * GROUP + n] for n in range(GROUP)]
            sums = [product(s) for s in slots]
            for s, value in zip(slots, sums):
                total[row[s]] += value

        @pl.loop(start + groups * GROUP, stop)
        def _(i):
            s = order[i]
            total[row[s]] += product(s)

        return stop

    lax.fori_loop(0, 4, quarter, 0)

    offset = 0
    out_copies = []
    for n, out in enumerate(outs):
        length = out.shape[0]
        copy = pltpu.make_async_copy(total.at[pl.ds(offset, length)], out, out_sem.at[n])
        copy.start()
        out_copies.append(copy)
        offset += length
    for copy in out_copies:
        copy.wait()


def slot_products(fill, blk, row, tiles, pieces):
    block = lambda n: jax.ShapeDtypeStruct((n, EDGE, WIDTH), jnp.float32)
    any_space = pl.BlockSpec(memory_space=pl.ANY)
    smem = pl.BlockSpec(memory_space=pltpu.SMEM)
    return pl.pallas_call(
        products_kernel,
        out_shape=[block(8), block(8), block(8), block(4), block(4)],
        in_specs=[smem] * 3 + [any_space] * (1 + len(pieces)),
        out_specs=[any_space] * 5,
        scratch_shapes=[
            pltpu.VMEM((BLOCKS * 4 * EDGE, WIDTH), jnp.float32),
            pltpu.VMEM((SLOTS, EDGE, EDGE), jnp.float32),
            pltpu.VMEM((BLOCKS, EDGE, WIDTH), jnp.float32),
            pltpu.SMEM((SLOTS,), jnp.int32),
            pltpu.SemaphoreType.DMA((BUCKETS,)),
            pltpu.SemaphoreType.DMA((len(pieces),)),
            pltpu.SemaphoreType.DMA((5,)),
        ],
        compiler_params=pltpu.CompilerParams(vmem_limit_bytes=48 * 1024 * 1024),
        cost_estimate=pl.CostEstimate(
            flops=2 * 3 * SLOTS * EDGE * EDGE * WIDTH, bytes_accessed=33 * 1024 * 1024, transcendentals=0
        ),
        name="slot_products",
    )(fill, blk, row, tiles, *pieces)


BAND = 64


def factor_kernel(gram, rows, embedding, factor, work):
    work[:, :WIDTH] = gram[...]
    work[:, WIDTH:] = rows[...].T
    lane = lax.broadcasted_iota(jnp.int32, (8, EDGE), 1)
    sub = lax.broadcasted_iota(jnp.int32, (8, EDGE), 0)
    columns = (WIDTH + EDGE) // EDGE
    for band in range(WIDTH // BAND):
        top = band * BAND
        lead = top // EDGE
        strips = BAND // 8
        held = [
            [work[top + 8 * s : top + 8 * s + 8, c * EDGE : (c + 1) * EDGE] for c in range(lead, columns)]
            for s in range(strips)
        ]
        for i in range(BAND):
            s0, r = divmod(i, 8)
            at = (top + i) % EDGE
            spread = [
                jnp.broadcast_to(held[s][0][:, at : at + 1], (8, EDGE)) for s in range(s0, strips)
            ]
            pivot = jnp.broadcast_to(spread[0][r : r + 1, :], (8, EDGE))
            inverse = 1.0 / pivot
            lines = [jnp.broadcast_to(v[r : r + 1, :], (8, EDGE)) for v in held[s0]]
            scaled = [v * inverse for v in lines]
            root = lax.rsqrt(pivot)
            for s in range(s0, strips):
                weight = spread[s - s0]
                if s == s0:
                    weight = jnp.where(sub > r, weight, 0.0)
                held[s] = [v - weight * w for v, w in zip(held[s], scaled)]
            held[s0] = [jnp.where(sub == r, w * root, v) for v, w in zip(held[s0], lines)]
        for s in range(strips):
            for c in range(lead, columns):
                value = held[s][c - lead]
                if c < WIDTH // EDGE:
                    value = jnp.where(lane + c * EDGE >= sub + (top + 8 * s), value, 0.0)
                work[top + 8 * s : top + 8 * s + 8, c * EDGE : (c + 1) * EDGE] = value
        below = top + BAND
        if below < WIDTH:
            base = below // EDGE * EDGE
            left = work[top:below, base:WIDTH]
            right = work[top:below, base:]
            update = lax.dot_general(
                left,
                right,
                (((0,), (0,)), ((), ())),
                precision=lax.Precision.HIGHEST,
                preferred_element_type=jnp.float32,
            )
            work[below:, base:] -= update[below - base :, :]
    scale = jnp.sqrt(jnp.float32(ROWS))
    for band in range(WIDTH // BAND):
        top = band * BAND
        lead = top // EDGE * EDGE
        if lead:
            factor[top : top + BAND, :lead] = jnp.zeros((BAND, lead), jnp.float32)
        factor[top : top + BAND, lead:] = work[top : top + BAND, lead:WIDTH] / scale
    embedding[...] = work[:, WIDTH:].T * scale


def factor_and_solve(gram, rows):
    vmem = pl.BlockSpec(memory_space=pltpu.VMEM)
    return pl.pallas_call(
        factor_kernel,
        out_shape=[
            jax.ShapeDtypeStruct((EDGE, WIDTH), jnp.float32),
            jax.ShapeDtypeStruct((WIDTH, WIDTH), jnp.float32),
        ],
        in_specs=[vmem, vmem],
        out_specs=[vmem, vmem],
        scratch_shapes=[pltpu.VMEM((WIDTH, WIDTH + EDGE), jnp.float32)],
        compiler_params=pltpu.CompilerParams(vmem_limit_bytes=16 * 1024 * 1024),
        name="factor_and_solve",
    )(gram, rows)


def exchange(value, axes):
    return lax.all_to_all(value, axes, 0, 0, tiled=True)


def on_device(tiles, tile_rows, tile_cols, bucket_fill, row_slot, sketch):
    here_x = lax.axis_index("x")
    here_z = lax.axis_index("z")

    slot_ids = jnp.arange(SLOTS, dtype=jnp.int32)
    bucket = slot_ids // PER_BUCKET
    cols = tile_cols[0, 0]
    far_x = (bucket // 8 - here_x) % 4
    far_z = (bucket % 8 - here_z) % 8
    blk = jnp.where(
        cols < 2, far_z * 8 + far_x * 2 + cols, 64 + far_x * 16 + far_z * 2 + (cols - 2)
    )
    block_ids = jnp.arange(BLOCKS, dtype=jnp.int32)
    target = jnp.sum(
        jnp.where(tile_rows[0, 0][:, None] == block_ids[None, :], row_slot[0][None, :], 0), axis=1
    )
    ahead = (target // 8 - here_x) % 4
    chunk = jnp.where(ahead == 3, 2, jnp.where(ahead == 2, 3, ahead))
    row = chunk * 8 + target % 8

    with jax.named_scope("gather"):
        half = sketch.shape[0] // 2
        along_x = ring_gather(sketch[:half], "x")
        along_z = ring_gather(sketch[half:], "z")
        slab = jnp.concatenate([part for block in along_x for part in block], axis=0)
        line = jnp.concatenate([part for block in along_z for part in block], axis=0)
        first = ring_gather(slab, "z")
        second = ring_gather(line, "x")
        pieces = [part for block in first + second for part in block]

    sums = slot_products(bucket_fill[0, 0], blk, row, tiles[0, 0], pieces)

    with jax.named_scope("scatter_rows"):
        own, up, down, far_up, far_down = sums
        from_below = shift(far_up, "x", 1)
        from_above = shift(far_down, "x", -1)
        up = jnp.concatenate([up[:4] + from_below, up[4:]], axis=0)
        down = jnp.concatenate([down[:4], down[4:] + from_above], axis=0)
        own = own + shift(up, "x", 1) + shift(down, "x", -1)
        product_rows = jnp.sum(exchange(own, "z"), axis=0)

    with jax.named_scope("gram"):
        gram = jnp.dot(
            product_rows.T,
            product_rows,
            precision=lax.Precision.HIGHEST,
            preferred_element_type=jnp.float32,
        )
        ring = ("y", "core", "x")
        part = jnp.sum(exchange(gram, ring).reshape(32, 8, WIDTH), axis=0)
        part = jnp.sum(
            exchange(jnp.broadcast_to(part[None], (8, 8, WIDTH)), "z"), axis=0
        )
        gram = exchange(jnp.broadcast_to(part[None], (32, 8, WIDTH)), ring).reshape(WIDTH, WIDTH)

    embedding, factor = factor_and_solve(gram, product_rows)
    return embedding, factor


def solution(mesh):
    fine = Mesh(mesh.devices.reshape(SIZES), AXES)
    grp, col = ("y", "core"), ("x", "z")
    placed = (
        P(grp, col, None, None, None),
        P(grp, col, None),
        P(grp, col, None),
        P(grp, col, None),
        P(grp, None),
        P(col, None),
    )
    return jax.shard_map(
        on_device,
        mesh=fine,
        in_specs=placed,
        out_specs=(P(AXES, None), P()),
        check_vma=False,
    )
```

```python
import functools

import jax
import jax.numpy as jnp
from jax import lax
from jax.experimental import pallas as pl
from jax.experimental.pallas import tpu as pltpu
from jax.sharding import Mesh
from jax.sharding import PartitionSpec as P

AXES = ("y", "core", "x", "z")
SIZES = (4, 2, 4, 8)
EDGE = 128
WIDTH = 256
BLOCKS = 32
BUCKETS = 32
PER_BUCKET = 6
SLOTS = 192
ROWS = 32768
GROUP = 4


def shift(value, axis, step):
    count = lax.axis_size(axis)
    return lax.ppermute(value, axis, [(i, (i + step) % count) for i in range(count)])


def ring_gather(block, axis):
    count = lax.axis_size(axis)
    found = [None] * count
    found[0] = (block,)
    behind = ahead = block
    for step in range(1, count // 2):
        behind = shift(behind, axis, 1)
        ahead = shift(ahead, axis, -1)
        found[count - step] = (behind,)
        found[step] = (ahead,)
    half = block.shape[0] // 2
    found[count // 2] = (shift(behind[:half], axis, 1), shift(ahead[half:], axis, -1))
    return found


def join(blocks):
    return jnp.concatenate([part for block in blocks for part in block], axis=0)


def products_kernel(part, fill, blk, side, row, tiles, *refs):
    if part == 0:
        first, second, total = refs[:3]
        panels, held, order, tile_sem, piece_sem = refs[3:]
    else:
        first, second, before, total = refs[:4]
        panels, held, order, tile_sem, piece_sem, before_sem = refs[4:]
    length = first.shape[0]
    copies = [
        pltpu.make_async_copy(first, panels.at[pl.ds(0, length)], piece_sem.at[0]),
        pltpu.make_async_copy(second, panels.at[pl.ds(length, length)], piece_sem.at[1]),
    ]
    if part == 1:
        copies.append(pltpu.make_async_copy(before, total, before_sem))
    for copy in copies:
        copy.start()

    def tile_copy(i):
        return pltpu.make_async_copy(tiles.at[order[i]], held.at[i], tile_sem.at[i])

    def list_bucket(b, count):
        def put(j, c):
            slot = b * PER_BUCKET + j
            wanted = side[slot] == part

            @pl.when(wanted)
            def _():
                order[c] = slot
                tile_copy(c).start()

            return c + wanted.astype(jnp.int32)

        return lax.fori_loop(0, fill[b], put, count)

    count = lax.fori_loop(0, BUCKETS, list_bucket, 0)
    if part == 0:
        total[...] = jnp.zeros_like(total)

    def product(i):
        tile = held[i]
        panel = panels[pl.ds(pl.multiple_of(blk[order[i]] * EDGE, EDGE), EDGE), :]
        tile_hi = tile.astype(jnp.bfloat16)
        tile_lo = (tile - tile_hi.astype(jnp.float32)).astype(jnp.bfloat16)
        panel_hi = panel.astype(jnp.bfloat16)
        panel_lo = (panel - panel_hi.astype(jnp.float32)).astype(jnp.bfloat16)
        left = jnp.concatenate([tile_hi, tile_hi, tile_lo], axis=1)
        right = jnp.concatenate([panel_hi, panel_lo, panel_hi], axis=0)
        return jnp.dot(left, right, preferred_element_type=jnp.float32)

    for copy in copies:
        copy.wait()
    groups = count // GROUP

    @pl.loop(0, groups)
    def _(g):
        slots = [g * GROUP + n for n in range(GROUP)]
        for i in slots:
            tile_copy(i).wait()
        sums = [product(i) for i in slots]
        for i, value in zip(slots, sums):
            total[row[order[i]]] += value

    @pl.loop(groups * GROUP, count)
    def _(i):
        tile_copy(i).wait()
        total[row[order[i]]] += product(i)


def slot_products(part, tables, tiles, pieces, before=None):
    any_space = pl.BlockSpec(memory_space=pl.ANY)
    smem = pl.BlockSpec(memory_space=pltpu.SMEM)
    vmem = pl.BlockSpec(memory_space=pltpu.VMEM)
    arrays = [tiles, *pieces] + ([before] if part else [])
    scratch = [
        pltpu.VMEM((2 * pieces[0].shape[0], WIDTH), jnp.float32),
        pltpu.VMEM((SLOTS, EDGE, EDGE), jnp.float32),
        pltpu.SMEM((SLOTS,), jnp.int32),
        pltpu.SemaphoreType.DMA((SLOTS,)),
        pltpu.SemaphoreType.DMA((2,)),
    ]
    if part:
        scratch.append(pltpu.SemaphoreType.DMA)
    return pl.pallas_call(
        functools.partial(products_kernel, part),
        out_shape=jax.ShapeDtypeStruct((BLOCKS, EDGE, WIDTH), jnp.float32),
        in_specs=[smem] * 4 + [any_space] * len(arrays),
        out_specs=vmem,
        scratch_shapes=scratch,
        compiler_params=pltpu.CompilerParams(vmem_limit_bytes=40 * 1024 * 1024),
        cost_estimate=pl.CostEstimate(
            flops=3 * SLOTS * EDGE * EDGE * WIDTH, bytes_accessed=22 * 1024 * 1024, transcendentals=0
        ),
        name="slot_products",
    )(*tables, *arrays)


BAND = 64


def factor_kernel(gram, rows, embedding, factor, work):
    work[:, :WIDTH] = gram[...]
    work[:, WIDTH:] = rows[...].T
    lane = lax.broadcasted_iota(jnp.int32, (8, EDGE), 1)
    sub = lax.broadcasted_iota(jnp.int32, (8, EDGE), 0)
    columns = (WIDTH + EDGE) // EDGE

    def along_lanes(value, at):
        return jnp.broadcast_to(value[:, at : at + 1], (8, EDGE))

    def along_rows(value, at):
        return jnp.broadcast_to(value[at : at + 1, :], (8, EDGE))

    for band in range(WIDTH // BAND):
        top = band * BAND
        lead = top // EDGE
        strips = BAND // 8
        held = [
            [work[top + 8 * s : top + 8 * s + 8, c * EDGE : (c + 1) * EDGE] for c in range(lead, columns)]
            for s in range(strips)
        ]
        for s0 in range(strips):
            at = (top + 8 * s0) % EDGE
            cols = {s: [along_lanes(held[s][0], at + q) for q in range(8)] for s in range(s0, strips)}
            block = {(t, r): along_rows(cols[s0][r], t) for t in range(8) for r in range(t + 1)}
            lower = {}
            inverse = []
            root = []
            for q in range(8):
                inverse.append(1.0 / block[q, q])
                root.append(lax.rsqrt(block[q, q]))
                for t in range(q + 1, 8):
                    lower[t, q] = block[t, q] * inverse[q]
                for t in range(q + 1, 8):
                    for r in range(q + 1, t + 1):
                        block[t, r] = block[t, r] - lower[t, q] * block[r, q]
            lines = []
            for q in range(8):
                line = [along_rows(v, q) for v in held[s0]]
                for t in range(q):
                    line = [v - lower[q, t] * w for v, w in zip(line, lines[t])]
                lines.append(line)
            for s in range(s0 + 1, strips):
                weights = []
                for q in range(8):
                    value = cols[s][q]
                    for t in range(q):
                        value = value - lower[q, t] * weights[t]
                    weights.append(value)
                weights = [v * w for v, w in zip(weights, inverse)]
                for q in range(8):
                    held[s] = [v - weights[q] * w for v, w in zip(held[s], lines[q])]
            final = [jnp.zeros((8, EDGE), jnp.float32)] * len(held[s0])
            for q in range(8):
                final = [jnp.where(sub == q, w * root[q], v) for v, w in zip(final, lines[q])]
            for c in range(lead, columns):
                value = final[c - lead]
                if c < WIDTH // EDGE:
                    value = jnp.where(lane + c * EDGE >= sub + (top + 8 * s0), value, 0.0)
                work[top + 8 * s0 : top + 8 * s0 + 8, c * EDGE : (c + 1) * EDGE] = value
        below = top + BAND
        if below < WIDTH:
            base = below // EDGE * EDGE
            left = work[top:below, base:WIDTH]
            right = work[top:below, base:]
            update = lax.dot_general(
                left,
                right,
                (((0,), (0,)), ((), ())),
                precision=lax.Precision.HIGHEST,
                preferred_element_type=jnp.float32,
            )
            work[below:, base:] -= update[below - base :, :]
    scale = jnp.sqrt(jnp.float32(ROWS))
    for band in range(WIDTH // BAND):
        top = band * BAND
        lead = top // EDGE * EDGE
        if lead:
            factor[top : top + BAND, :lead] = jnp.zeros((BAND, lead), jnp.float32)
        factor[top : top + BAND, lead:] = work[top : top + BAND, lead:WIDTH] / scale
    embedding[...] = work[:, WIDTH:].T * scale


def factor_and_solve(gram, rows):
    vmem = pl.BlockSpec(memory_space=pltpu.VMEM)
    return pl.pallas_call(
        factor_kernel,
        out_shape=[
            jax.ShapeDtypeStruct((EDGE, WIDTH), jnp.float32),
            jax.ShapeDtypeStruct((WIDTH, WIDTH), jnp.float32),
        ],
        in_specs=[vmem, vmem],
        out_specs=[vmem, vmem],
        scratch_shapes=[pltpu.VMEM((WIDTH, WIDTH + EDGE), jnp.float32)],
        compiler_params=pltpu.CompilerParams(vmem_limit_bytes=16 * 1024 * 1024),
        name="factor_and_solve",
    )(gram, rows)


def exchange(value, axes):
    return lax.all_to_all(value, axes, 0, 0, tiled=True)


def on_device(tiles, tile_rows, tile_cols, bucket_fill, row_slot, sketch):
    here_x = lax.axis_index("x")
    here_z = lax.axis_index("z")
    here_core = lax.axis_index("core")

    slot_ids = jnp.arange(SLOTS, dtype=jnp.int32)
    bucket = slot_ids // PER_BUCKET
    cols = tile_cols[0, 0]
    far_x = (bucket // 8 - here_x) % 4
    far_z = (bucket % 8 - here_z) % 8
    blk = jnp.where(cols % 2 == 0, far_z * 4 + far_x, 32 + far_x * 8 + far_z)
    side = (cols // 2 + here_core) % 2
    block_ids = jnp.arange(BLOCKS, dtype=jnp.int32)
    target = jnp.sum(
        jnp.where(tile_rows[0, 0][:, None] == block_ids[None, :], row_slot[0][None, :], 0), axis=1
    )
    ahead = (target // 8 - here_x) % 4
    chunk = jnp.where(ahead == 3, 2, jnp.where(ahead == 2, 3, ahead))
    row = chunk * 8 + target % 8

    with jax.named_scope("gather"):
        mine = lax.dynamic_slice_in_dim(sketch, here_core * 2 * EDGE, 2 * EDGE, 0)
        slab = join(ring_gather(mine[:EDGE], "x"))
        line = join(ring_gather(mine[EDGE:], "z"))
        first = join(ring_gather(slab, "z"))
        second = join(ring_gather(line, "x"))
        first_other = shift(first, "core", 1)
        second_other = shift(second, "core", 1)

    tables = (bucket_fill[0, 0], blk, side, row)
    sums = slot_products(0, tables, tiles[0, 0], (first, second))
    sums = slot_products(1, tables, tiles[0, 0], (first_other, second_other), sums)

    with jax.named_scope("scatter_rows"):
        own, up, down, far_up, far_down = (
            sums[:8], sums[8:16], sums[16:24], sums[24:28], sums[28:32]
        )
        from_below = shift(far_up, "x", 1)
        from_above = shift(far_down, "x", -1)
        up = jnp.concatenate([up[:4] + from_below, up[4:]], axis=0)
        down = jnp.concatenate([down[:4], down[4:] + from_above], axis=0)
        own = own + shift(up, "x", 1) + shift(down, "x", -1)
        product_rows = jnp.sum(exchange(own, "z"), axis=0)

    with jax.named_scope("gram"):
        gram = jnp.dot(
            product_rows.T,
            product_rows,
            precision=lax.Precision.HIGHEST,
            preferred_element_type=jnp.float32,
        )
        ring = ("y", "core", "x")
        part = jnp.sum(exchange(gram, ring).reshape(32, 8, WIDTH), axis=0)
        part = jnp.sum(
            exchange(jnp.broadcast_to(part[None], (8, 8, WIDTH)), "z"), axis=0
        )
        gram = exchange(jnp.broadcast_to(part[None], (32, 8, WIDTH)), ring).reshape(WIDTH, WIDTH)

    embedding, factor = factor_and_solve(gram, product_rows)
    return embedding, factor


def solution(mesh):
    fine = Mesh(mesh.devices.reshape(SIZES), AXES)
    grp, col = ("y", "core"), ("x", "z")
    placed = (
        P(grp, col, None, None, None),
        P(grp, col, None),
        P(grp, col, None),
        P(grp, col, None),
        P(grp, None),
        P(col, None),
    )
    return jax.shard_map(
        on_device,
        mesh=fine,
        in_specs=placed,
        out_specs=(P(AXES, None), P()),
        check_vma=False,
    )
```

```python
import functools

import jax
import jax.numpy as jnp
from jax import lax
from jax.experimental import pallas as pl
from jax.experimental.pallas import tpu as pltpu
from jax.sharding import Mesh
from jax.sharding import PartitionSpec as P

AXES = ("y", "core", "x", "z")
SIZES = (4, 2, 4, 8)
EDGE = 128
WIDTH = 256
BLOCKS = 32
BUCKETS = 32
PER_BUCKET = 6
SLOTS = 192
ROWS = 32768
GROUP = 8
LIMIT = 16


def shift(value, axis, step):
    count = lax.axis_size(axis)
    return lax.ppermute(value, axis, [(i, (i + step) % count) for i in range(count)])


def both_ways(up, down, axis, step=1):
    up, down = lax.optimization_barrier((up, down))
    return lax.optimization_barrier((shift(up, axis, step), shift(down, axis, -step)))


def join_rows(top, bottom):
    return jnp.concatenate([top, bottom], axis=0)


def ring_gather(block, axis):
    count = lax.axis_size(axis)
    found = [None] * count
    found[0] = (block,)
    behind = ahead = block
    for step in range(1, count // 2):
        behind = shift(behind, axis, 1)
        ahead = shift(ahead, axis, -1)
        found[count - step] = (behind,)
        found[step] = (ahead,)
    half = block.shape[0] // 2
    found[count // 2] = (shift(behind[:half], axis, 1), shift(ahead[half:], axis, -1))
    return found


def join_kernel(*refs):
    out = refs[-1]
    offset = 0
    for piece in refs[:-1]:
        length = piece.shape[0]
        out[pl.ds(offset, length), :] = piece[...]
        offset += length


def join(blocks):
    pieces = [part for block in blocks for part in block]
    total = sum(piece.shape[0] for piece in pieces)
    vmem = pl.BlockSpec(memory_space=pltpu.VMEM)
    return pl.pallas_call(
        join_kernel,
        out_shape=jax.ShapeDtypeStruct((total, WIDTH), jnp.float32),
        in_specs=[vmem] * len(pieces),
        out_specs=vmem,
        compiler_params=pltpu.CompilerParams(vmem_limit_bytes=LIMIT * 1024 * 1024),
        cost_estimate=pl.CostEstimate(flops=0, bytes_accessed=total * WIDTH * 8, transcendentals=0),
        name="join",
    )(*pieces)


def products_kernel(part, fill, blk, side, row, tiles, panels, *refs):
    if part == 0:
        total, order = refs
    else:
        before, total, order = refs

    def list_bucket(b, count):
        def put(j, c):
            slot = b * PER_BUCKET + j
            order[c] = slot
            return c + (side[slot] == part).astype(jnp.int32)

        return lax.fori_loop(0, fill[b], put, count)

    count = lax.fori_loop(0, BUCKETS, list_bucket, 0)
    total[...] = before[...] if part else jnp.zeros_like(total)

    def product(slot):
        tile = tiles[slot]
        panel = panels[pl.ds(pl.multiple_of(blk[slot] * EDGE, EDGE), EDGE), :]
        tile_hi = tile.astype(jnp.bfloat16)
        tile_lo = (tile - tile_hi.astype(jnp.float32)).astype(jnp.bfloat16)
        panel_hi = panel.astype(jnp.bfloat16)
        panel_lo = (panel - panel_hi.astype(jnp.float32)).astype(jnp.bfloat16)
        left = jnp.concatenate([tile_hi, tile_hi, tile_lo], axis=1)
        right = jnp.concatenate([panel_hi, panel_lo, panel_hi], axis=0)
        return jnp.dot(left, right, preferred_element_type=jnp.float32)

    groups = count // GROUP

    @pl.loop(0, groups)
    def _(g):
        slots = [order[g * GROUP + n] for n in range(GROUP)]
        sums = [product(s) for s in slots]
        for s, value in zip(slots, sums):
            total[row[s]] += value

    @pl.loop(groups * GROUP, count)
    def _(i):
        s = order[i]
        total[row[s]] += product(s)


def slot_products(part, tables, tiles, panels, before=None):
    smem = pl.BlockSpec(memory_space=pltpu.SMEM)
    vmem = pl.BlockSpec(memory_space=pltpu.VMEM)
    arrays = [tiles, panels] + ([before] if part else [])
    return pl.pallas_call(
        functools.partial(products_kernel, part),
        out_shape=jax.ShapeDtypeStruct((BLOCKS, EDGE, WIDTH), jnp.float32),
        in_specs=[smem] * 4 + [vmem] * len(arrays),
        out_specs=vmem,
        input_output_aliases={6: 0} if part else {},
        scratch_shapes=[pltpu.SMEM((SLOTS,), jnp.int32)],
        compiler_params=pltpu.CompilerParams(vmem_limit_bytes=LIMIT * 1024 * 1024),
        cost_estimate=pl.CostEstimate(
            flops=3 * SLOTS * EDGE * EDGE * WIDTH, bytes_accessed=22 * 1024 * 1024, transcendentals=0
        ),
        name="slot_products",
    )(*tables, *arrays)


BAND = 64


def factor_kernel(gram, rows, embedding, factor, work):
    work[:, :WIDTH] = gram[...]
    work[:, WIDTH:] = rows[...].T
    lane = lax.broadcasted_iota(jnp.int32, (8, EDGE), 1)
    sub = lax.broadcasted_iota(jnp.int32, (8, EDGE), 0)
    columns = (WIDTH + EDGE) // EDGE

    def along_lanes(value, at):
        return jnp.broadcast_to(value[:, at : at + 1], (8, EDGE))

    def along_rows(value, at):
        return jnp.broadcast_to(value[at : at + 1, :], (8, EDGE))

    for band in range(WIDTH // BAND):
        top = band * BAND
        lead = top // EDGE
        strips = BAND // 8
        held = [
            [work[top + 8 * s : top + 8 * s + 8, c * EDGE : (c + 1) * EDGE] for c in range(lead, columns)]
            for s in range(strips)
        ]
        for s0 in range(strips):
            at = (top + 8 * s0) % EDGE
            cols = {s: [along_lanes(held[s][0], at + q) for q in range(8)] for s in range(s0, strips)}
            block = {(t, r): along_rows(cols[s0][r], t) for t in range(8) for r in range(t + 1)}
            lower = {}
            inverse = []
            root = []
            for q in range(8):
                inverse.append(1.0 / block[q, q])
                root.append(lax.rsqrt(block[q, q]))
                for t in range(q + 1, 8):
                    lower[t, q] = block[t, q] * inverse[q]
                for t in range(q + 1, 8):
                    for r in range(q + 1, t + 1):
                        block[t, r] = block[t, r] - lower[t, q] * block[r, q]
            lines = []
            for q in range(8):
                line = [along_rows(v, q) for v in held[s0]]
                for t in range(q):
                    line = [v - lower[q, t] * w for v, w in zip(line, lines[t])]
                lines.append(line)
            for s in range(s0 + 1, strips):
                weights = []
                for q in range(8):
                    value = cols[s][q]
                    for t in range(q):
                        value = value - lower[q, t] * weights[t]
                    weights.append(value)
                weights = [v * w for v, w in zip(weights, inverse)]
                for q in range(8):
                    held[s] = [v - weights[q] * w for v, w in zip(held[s], lines[q])]
            final = [jnp.zeros((8, EDGE), jnp.float32)] * len(held[s0])
            for q in range(8):
                final = [jnp.where(sub == q, w * root[q], v) for v, w in zip(final, lines[q])]
            for c in range(lead, columns):
                value = final[c - lead]
                if c < WIDTH // EDGE:
                    value = jnp.where(lane + c * EDGE >= sub + (top + 8 * s0), value, 0.0)
                work[top + 8 * s0 : top + 8 * s0 + 8, c * EDGE : (c + 1) * EDGE] = value
        below = top + BAND
        if below < WIDTH:
            base = below // EDGE * EDGE
            left = work[top:below, base:WIDTH]
            right = work[top:below, base:]
            update = lax.dot_general(
                left,
                right,
                (((0,), (0,)), ((), ())),
                precision=lax.Precision.HIGHEST,
                preferred_element_type=jnp.float32,
            )
            work[below:, base:] -= update[below - base :, :]
    scale = jnp.sqrt(jnp.float32(ROWS))
    for band in range(WIDTH // BAND):
        top = band * BAND
        lead = top // EDGE * EDGE
        if lead:
            factor[top : top + BAND, :lead] = jnp.zeros((BAND, lead), jnp.float32)
        factor[top : top + BAND, lead:] = work[top : top + BAND, lead:WIDTH] / scale
    embedding[...] = work[:, WIDTH:].T * scale


def factor_and_solve(gram, rows):
    vmem = pl.BlockSpec(memory_space=pltpu.VMEM)
    return pl.pallas_call(
        factor_kernel,
        out_shape=[
            jax.ShapeDtypeStruct((EDGE, WIDTH), jnp.float32),
            jax.ShapeDtypeStruct((WIDTH, WIDTH), jnp.float32),
        ],
        in_specs=[vmem, vmem],
        out_specs=[vmem, vmem],
        scratch_shapes=[pltpu.VMEM((WIDTH, WIDTH + EDGE), jnp.float32)],
        compiler_params=pltpu.CompilerParams(vmem_limit_bytes=16 * 1024 * 1024),
        name="factor_and_solve",
    )(gram, rows)


def exchange(value, axes):
    return lax.all_to_all(value, axes, 0, 0, tiled=True)


def on_device(tiles, tile_rows, tile_cols, bucket_fill, row_slot, sketch):
    here_x = lax.axis_index("x")
    here_z = lax.axis_index("z")
    here_core = lax.axis_index("core")

    slot_ids = jnp.arange(SLOTS, dtype=jnp.int32)
    bucket = slot_ids // PER_BUCKET
    cols = tile_cols[0, 0]
    far_x = (bucket // 8 - here_x) % 4
    far_z = (bucket % 8 - here_z) % 8
    blk = jnp.where(cols % 2 == 0, far_z * 4 + far_x, 32 + far_x * 8 + far_z)
    side = (cols // 2 + here_core) % 2
    block_ids = jnp.arange(BLOCKS, dtype=jnp.int32)
    target = jnp.sum(
        jnp.where(tile_rows[0, 0][:, None] == block_ids[None, :], row_slot[0][None, :], 0), axis=1
    )
    ahead = (target // 8 - here_x) % 4
    chunk = jnp.where(ahead == 3, 2, jnp.where(ahead == 2, 3, ahead))
    row = chunk * 8 + (target % 8 - here_z) % 8

    with jax.named_scope("gather"):
        mine = lax.dynamic_slice_in_dim(sketch, here_core * 2 * EDGE, 2 * EDGE, 0)
        slab = join(ring_gather(mine[:EDGE], "x"))
        line = join(ring_gather(mine[EDGE:], "z"))
        panels = join(ring_gather(slab, "z") + ring_gather(line, "x"))
        panels_other = shift(panels, "core", 1)

    tables = (bucket_fill[0, 0], blk, side, row)
    sums = slot_products(0, tables, tiles[0, 0], panels)
    sums = slot_products(1, tables, tiles[0, 0], panels_other, sums)

    with jax.named_scope("scatter_rows"):
        own, up, down = sums[:8], sums[8:16], sums[16:24]
        far_up, far_down = sums[24:28], sums[28:32]
        from_below, from_above = both_ways(far_up, far_down, "x")
        up = jnp.concatenate([up[:4] + from_below, up[4:]], axis=0)
        down = jnp.concatenate([down[:4], down[4:] + from_above], axis=0)
        from_below, from_above = both_ways(up, down, "x")
        own = own + from_below + from_above
        half = EDGE // 2
        from_below, from_above = both_ways(own[4, :half], own[4, half:], "z")
        up = jnp.stack([own[2], join_rows(own[3, :half] + from_below, own[3, half:])])
        down = jnp.stack([own[6], join_rows(own[5, :half], own[5, half:] + from_above)])
        from_below, from_above = both_ways(up, down, "z", 2)
        up = own[1] + from_below[1]
        down = own[7] + from_above[1]
        middle = own[0] + from_below[0] + from_above[0]
        from_below, from_above = both_ways(up, down, "z")
        product_rows = middle + from_below + from_above

    with jax.named_scope("gram"):
        gram = jnp.dot(
            product_rows.T,
            product_rows,
            precision=lax.Precision.HIGHEST,
            preferred_element_type=jnp.float32,
        )
        ring = ("y", "core", "x")
        part = jnp.sum(exchange(gram, ring).reshape(32, 8, WIDTH), axis=0)
        part = jnp.sum(
            exchange(jnp.broadcast_to(part[None], (8, 8, WIDTH)), "z"), axis=0
        )
        gram = exchange(jnp.broadcast_to(part[None], (32, 8, WIDTH)), ring).reshape(WIDTH, WIDTH)

    embedding, factor = factor_and_solve(gram, product_rows)
    return embedding, factor


def solution(mesh):
    fine = Mesh(mesh.devices.reshape(SIZES), AXES)
    grp, col = ("y", "core"), ("x", "z")
    placed = (
        P(grp, col, None, None, None),
        P(grp, col, None),
        P(grp, col, None),
        P(grp, col, None),
        P(grp, None),
        P(col, None),
    )
    return jax.shard_map(
        on_device,
        mesh=fine,
        in_specs=placed,
        out_specs=(P(AXES, None), P()),
        check_vma=False,
    )
```

```python
import functools

import jax
import jax.numpy as jnp
from jax import lax
from jax.experimental import pallas as pl
from jax.experimental.pallas import tpu as pltpu
from jax.sharding import Mesh
from jax.sharding import PartitionSpec as P

AXES = ("y", "core", "x", "z")
SIZES = (4, 2, 4, 8)
EDGE = 128
WIDTH = 256
BLOCKS = 32
BUCKETS = 32
PER_BUCKET = 6
SLOTS = 192
ROWS = 32768
GROUP = 8
LIMIT = 32
FAR_ROW = 24


def shift(value, axis, step):
    count = lax.axis_size(axis)
    return lax.ppermute(value, axis, [(i, (i + step) % count) for i in range(count)])


def both_ways(up, down, axis, step=1):
    up, down = lax.optimization_barrier((up, down))
    return lax.optimization_barrier((shift(up, axis, step), shift(down, axis, -step)))


def join_rows(top, bottom):
    return jnp.concatenate([top, bottom], axis=0)


def ring_gather(block, axis, beside=()):
    count = lax.axis_size(axis)
    found = [None] * count
    found[0] = (block,)
    behind = ahead = block
    for step in range(1, count // 2):
        behind = shift(behind, axis, 1)
        ahead = shift(ahead, axis, -1)
        found[count - step] = (behind,)
        found[step] = (ahead,)
    half = block.shape[0] // 2
    if beside:
        behind, ahead, beside = lax.optimization_barrier((behind, ahead, beside))
    found[count // 2] = (shift(behind[:half], axis, 1), shift(ahead[half:], axis, -1))
    return (found, *beside) if beside else found


def join_kernel(*refs):
    out = refs[-1]
    offset = 0
    for piece in refs[:-1]:
        length = piece.shape[0]
        out[pl.ds(offset, length), :] = piece[...]
        offset += length


def join(blocks):
    pieces = [part for block in blocks for part in block]
    total = sum(piece.shape[0] for piece in pieces)
    vmem = pl.BlockSpec(memory_space=pltpu.VMEM)
    return pl.pallas_call(
        join_kernel,
        out_shape=jax.ShapeDtypeStruct((total, WIDTH), jnp.float32),
        in_specs=[vmem] * len(pieces),
        out_specs=vmem,
        compiler_params=pltpu.CompilerParams(vmem_limit_bytes=LIMIT * 1024 * 1024),
        cost_estimate=pl.CostEstimate(flops=0, bytes_accessed=total * WIDTH * 8, transcendentals=0),
        name="join",
    )(*pieces)


def plan_kernel(fill, kind, *refs):
    plan, counts = refs[:3], refs[3]

    def list_bucket(b, ends):
        def put(j, ends):
            slot = b * PER_BUCKET + j
            which = kind[slot]
            for k in range(3):
                plan[k][ends[k]] = slot
            return tuple(e + (which == k).astype(jnp.int32) for k, e in enumerate(ends))

        return lax.fori_loop(0, fill[b], put, ends)

    ends = lax.fori_loop(0, BUCKETS, list_bucket, (0, 0, 0))
    for k in range(3):
        counts[k] = ends[k]


def slot_plan(fill, kind):
    smem = pl.BlockSpec(memory_space=pltpu.SMEM)
    return pl.pallas_call(
        plan_kernel,
        out_shape=[jax.ShapeDtypeStruct((SLOTS,), jnp.int32)] * 3
        + [jax.ShapeDtypeStruct((3,), jnp.int32)],
        in_specs=[smem, smem],
        out_specs=[smem] * 4,
        cost_estimate=pl.CostEstimate(flops=0, bytes_accessed=12 * 1024 * 1024, transcendentals=0),
        name="slot_plan",
    )(fill, kind)


def products_kernel(part, counts, listed, blk, row, tiles, panels, *refs):
    first_row = FAR_ROW if part == 1 else 0
    if part == 0:
        total, held, tile_sem = refs
    else:
        before, outs = refs[0], refs[1:-3]
        total, held, tile_sem = refs[-3:]
    count = counts[part]

    def tile_copy(i):
        return pltpu.make_async_copy(tiles.at[listed[i]], held.at[i], tile_sem.at[i])

    @pl.loop(0, count)
    def _(i):
        tile_copy(i).start()

    total[...] = before[first_row : first_row + total.shape[0]] if part else jnp.zeros_like(total)

    def product(i):
        slot = listed[i]
        tile = held[i]
        panel = panels[pl.ds(pl.multiple_of(blk[slot] * EDGE, EDGE), EDGE), :]
        tile_hi = tile.astype(jnp.bfloat16)
        tile_lo = (tile - tile_hi.astype(jnp.float32)).astype(jnp.bfloat16)
        panel_hi = panel.astype(jnp.bfloat16)
        panel_lo = (panel - panel_hi.astype(jnp.float32)).astype(jnp.bfloat16)
        left = jnp.concatenate([tile_hi, tile_hi, tile_lo], axis=1)
        right = jnp.concatenate([panel_hi, panel_lo, panel_hi], axis=0)
        return jnp.dot(left, right, preferred_element_type=jnp.float32)

    groups = count // GROUP

    @pl.loop(0, groups)
    def _(g):
        slots = [g * GROUP + n for n in range(GROUP)]
        for i in slots:
            tile_copy(i).wait()
        sums = [product(i) for i in slots]
        for i, value in zip(slots, sums):
            total[row[listed[i]] - first_row] += value

    @pl.loop(groups * GROUP, count)
    def _(i):
        tile_copy(i).wait()
        total[row[listed[i]] - first_row] += product(i)

    if part:
        offset = 0
        for out in outs:
            length = out.shape[0]
            out[...] = total[offset : offset + length]
            offset += length


def slot_products(part, tables, tiles, panels, before=None):
    any_space = pl.BlockSpec(memory_space=pl.ANY)
    smem = pl.BlockSpec(memory_space=pltpu.SMEM)
    vmem = pl.BlockSpec(memory_space=pltpu.VMEM)
    block = lambda n: jax.ShapeDtypeStruct((n, EDGE, WIDTH), jnp.float32)
    scratch = [pltpu.VMEM((SLOTS, EDGE, EDGE), jnp.float32), pltpu.SemaphoreType.DMA((SLOTS,))]
    arrays = [tiles, panels]
    if part == 0:
        shapes = [block(BLOCKS)]
    else:
        shapes = [block(4), block(4)] if part == 1 else [block(8)] + [block(4)] * 4
        rows = BLOCKS - FAR_ROW if part == 1 else FAR_ROW
        scratch = [pltpu.VMEM((rows, EDGE, WIDTH), jnp.float32)] + scratch
        arrays.append(before)
    share = (4, 1, 3)[part]
    return pl.pallas_call(
        functools.partial(products_kernel, part),
        out_shape=shapes,
        in_specs=[smem] * 4 + [any_space] + [vmem] * (len(arrays) - 1),
        out_specs=[vmem] * len(shapes),
        scratch_shapes=scratch,
        compiler_params=pltpu.CompilerParams(vmem_limit_bytes=LIMIT * 1024 * 1024),
        cost_estimate=pl.CostEstimate(
            flops=share * SLOTS * EDGE * EDGE * WIDTH,
            bytes_accessed=share * 3 * 1024 * 1024,
            transcendentals=0,
        ),
        name="slot_products",
    )(*tables, *arrays)


BAND = 64


def factor_kernel(gram, rows, embedding, factor, work):
    work[:, :WIDTH] = gram[...]
    work[:, WIDTH:] = rows[...].T
    lane = lax.broadcasted_iota(jnp.int32, (8, EDGE), 1)
    sub = lax.broadcasted_iota(jnp.int32, (8, EDGE), 0)
    columns = (WIDTH + EDGE) // EDGE

    def along_lanes(value, at):
        return jnp.broadcast_to(value[:, at : at + 1], (8, EDGE))

    def along_rows(value, at):
        return jnp.broadcast_to(value[at : at + 1, :], (8, EDGE))

    for band in range(WIDTH // BAND):
        top = band * BAND
        lead = top // EDGE
        strips = BAND // 8
        held = [
            [work[top + 8 * s : top + 8 * s + 8, c * EDGE : (c + 1) * EDGE] for c in range(lead, columns)]
            for s in range(strips)
        ]
        for s0 in range(strips):
            at = (top + 8 * s0) % EDGE
            cols = {s: [along_lanes(held[s][0], at + q) for q in range(8)] for s in range(s0, strips)}
            block = {(t, r): along_rows(cols[s0][r], t) for t in range(8) for r in range(t + 1)}
            lower = {}
            inverse = []
            root = []
            for q in range(8):
                inverse.append(1.0 / block[q, q])
                root.append(lax.rsqrt(block[q, q]))
                for t in range(q + 1, 8):
                    lower[t, q] = block[t, q] * inverse[q]
                for t in range(q + 1, 8):
                    for r in range(q + 1, t + 1):
                        block[t, r] = block[t, r] - lower[t, q] * block[r, q]
            lines = []
            for q in range(8):
                line = [along_rows(v, q) for v in held[s0]]
                for t in range(q):
                    line = [v - lower[q, t] * w for v, w in zip(line, lines[t])]
                lines.append(line)
            for s in range(s0 + 1, strips):
                weights = []
                for q in range(8):
                    value = cols[s][q]
                    for t in range(q):
                        value = value - lower[q, t] * weights[t]
                    weights.append(value)
                weights = [v * w for v, w in zip(weights, inverse)]
                for q in range(8):
                    held[s] = [v - weights[q] * w for v, w in zip(held[s], lines[q])]
            final = [jnp.zeros((8, EDGE), jnp.float32)] * len(held[s0])
            for q in range(8):
                final = [jnp.where(sub == q, w * root[q], v) for v, w in zip(final, lines[q])]
            for c in range(lead, columns):
                value = final[c - lead]
                if c < WIDTH // EDGE:
                    value = jnp.where(lane + c * EDGE >= sub + (top + 8 * s0), value, 0.0)
                work[top + 8 * s0 : top + 8 * s0 + 8, c * EDGE : (c + 1) * EDGE] = value
        below = top + BAND
        if below < WIDTH:
            base = below // EDGE * EDGE
            left = work[top:below, base:WIDTH]
            right = work[top:below, base:]
            update = lax.dot_general(
                left,
                right,
                (((0,), (0,)), ((), ())),
                precision=lax.Precision.HIGHEST,
                preferred_element_type=jnp.float32,
            )
            work[below:, base:] -= update[below - base :, :]
    scale = jnp.sqrt(jnp.float32(ROWS))
    for band in range(WIDTH // BAND):
        top = band * BAND
        lead = top // EDGE * EDGE
        if lead:
            factor[top : top + BAND, :lead] = jnp.zeros((BAND, lead), jnp.float32)
        factor[top : top + BAND, lead:] = work[top : top + BAND, lead:WIDTH] / scale
    embedding[...] = work[:, WIDTH:].T * scale


def factor_and_solve(gram, rows):
    vmem = pl.BlockSpec(memory_space=pltpu.VMEM)
    return pl.pallas_call(
        factor_kernel,
        out_shape=[
            jax.ShapeDtypeStruct((EDGE, WIDTH), jnp.float32),
            jax.ShapeDtypeStruct((WIDTH, WIDTH), jnp.float32),
        ],
        in_specs=[vmem, vmem],
        out_specs=[vmem, vmem],
        scratch_shapes=[pltpu.VMEM((WIDTH, WIDTH + EDGE), jnp.float32)],
        compiler_params=pltpu.CompilerParams(vmem_limit_bytes=16 * 1024 * 1024),
        name="factor_and_solve",
    )(gram, rows)


def exchange(value, axes):
    return lax.all_to_all(value, axes, 0, 0, tiled=True)


def on_device(tiles, tile_rows, tile_cols, bucket_fill, row_slot, sketch):
    here_x = lax.axis_index("x")
    here_z = lax.axis_index("z")
    here_core = lax.axis_index("core")

    slot_ids = jnp.arange(SLOTS, dtype=jnp.int32)
    bucket = slot_ids // PER_BUCKET
    cols = tile_cols[0, 0]
    far_x = (bucket // 8 - here_x) % 4
    far_z = (bucket % 8 - here_z) % 8
    blk = jnp.where(cols % 2 == 0, far_z * 4 + far_x, 32 + far_x * 8 + far_z)
    side = (cols // 2 + here_core) % 2
    block_ids = jnp.arange(BLOCKS, dtype=jnp.int32)
    target = jnp.sum(
        jnp.where(tile_rows[0, 0][:, None] == block_ids[None, :], row_slot[0][None, :], 0), axis=1
    )
    ahead = (target // 8 - here_x) % 4
    chunk = jnp.where(ahead == 3, 2, jnp.where(ahead == 2, 3, ahead))
    row = chunk * 8 + (target % 8 - here_z) % 8
    kind = jnp.where(side == 0, 0, jnp.where(row >= FAR_ROW, 1, 2))

    with jax.named_scope("gather"):
        mine = lax.dynamic_slice_in_dim(sketch, here_core * 2 * EDGE, 2 * EDGE, 0)
        slab = join(ring_gather(mine[:EDGE], "x"))
        line = join(ring_gather(mine[EDGE:], "z"))
        second, *plan, counts = ring_gather(line, "x", slot_plan(bucket_fill[0, 0], kind))
        panels = join(ring_gather(slab, "z") + second)
        panels_other = shift(panels, "core", 1)

    stack = tiles[0, 0]
    tables = [(counts, listed, blk, row) for listed in plan]
    (sums,) = slot_products(0, tables[0], stack, panels)
    far = slot_products(1, tables[1], stack, panels_other, sums)
    near = slot_products(2, tables[2], stack, panels_other, sums)

    with jax.named_scope("scatter_rows"):
        far_below, far_above = shift(far[0], "x", 1), shift(far[1], "x", -1)
        own, up_low, up_high, down_low, down_high = near
        up_low = up_low + far_below
        down_high = down_high + far_above
        high_below, low_above = shift(up_high, "x", 1), shift(down_low, "x", -1)
        low_below, high_above = shift(up_low, "x", 1), shift(down_high, "x", -1)
        own = jnp.concatenate(
            [own[:4] + low_below + low_above, own[4:] + high_below + high_above], axis=0
        )
        half = EDGE // 2
        from_below, from_above = both_ways(own[4, :half], own[4, half:], "z")
        up = jnp.stack([own[2], join_rows(own[3, :half] + from_below, own[3, half:])])
        down = jnp.stack([own[6], join_rows(own[5, :half], own[5, half:] + from_above)])
        from_below, from_above = both_ways(up, down, "z", 2)
        up = own[1] + from_below[1]
        down = own[7] + from_above[1]
        middle = own[0] + from_below[0] + from_above[0]
        from_below, from_above = both_ways(up, down, "z")
        product_rows = middle + from_below + from_above

    with jax.named_scope("gram"):
        gram = jnp.dot(
            product_rows.T,
            product_rows,
            precision=lax.Precision.HIGHEST,
            preferred_element_type=jnp.float32,
        )
        ring = ("y", "core", "x")
        part = jnp.sum(exchange(gram, ring).reshape(32, 8, WIDTH), axis=0)
        part = jnp.sum(
            exchange(jnp.broadcast_to(part[None], (8, 8, WIDTH)), "z"), axis=0
        )
        gram = exchange(jnp.broadcast_to(part[None], (32, 8, WIDTH)), ring).reshape(WIDTH, WIDTH)

    embedding, factor = factor_and_solve(gram, product_rows)
    return embedding, factor


def solution(mesh):
    fine = Mesh(mesh.devices.reshape(SIZES), AXES)
    grp, col = ("y", "core"), ("x", "z")
    placed = (
        P(grp, col, None, None, None),
        P(grp, col, None),
        P(grp, col, None),
        P(grp, col, None),
        P(grp, None),
        P(col, None),
    )
    return jax.shard_map(
        on_device,
        mesh=fine,
        in_specs=placed,
        out_specs=(P(AXES, None), P()),
        check_vma=False,
    )
```

```python
import functools

import jax
import jax.numpy as jnp
from jax import lax
from jax.experimental import pallas as pl
from jax.experimental.pallas import tpu as pltpu
from jax.sharding import Mesh
from jax.sharding import PartitionSpec as P

AXES = ("y", "core", "x", "z")
SIZES = (4, 2, 4, 8)
EDGE = 128
WIDTH = 256
BLOCKS = 32
BUCKETS = 32
PER_BUCKET = 6
SLOTS = 192
ROWS = 32768
GROUP = 8
LIMIT = 32
FAR_ROW = 24


def shift(value, axis, step):
    count = lax.axis_size(axis)
    return lax.ppermute(value, axis, [(i, (i + step) % count) for i in range(count)])


def both_ways(up, down, axis, step=1):
    up, down = lax.optimization_barrier((up, down))
    return lax.optimization_barrier((shift(up, axis, step), shift(down, axis, -step)))


def join_rows(top, bottom):
    return jnp.concatenate([top, bottom], axis=0)


def ring_gather(block, axis, by_core=False):
    count = lax.axis_size(axis)
    found = [None] * count
    found[0] = (block,)
    behind = ahead = block
    for step in range(1, count // 2):
        behind = shift(behind, axis, 1)
        ahead = shift(ahead, axis, -1)
        found[count - step] = (behind,)
        found[step] = (ahead,)
    if by_core:
        pairs = [
            (core * count + i, core * count + (i + 1 - 2 * core) % count)
            for core in range(2)
            for i in range(count)
        ]
        value = jnp.where(lax.axis_index("core") == 0, behind, ahead)
        found[count // 2] = (lax.ppermute(value, ("core", axis), pairs),)
    else:
        half = block.shape[0] // 2
        found[count // 2] = (shift(behind[:half], axis, 1), shift(ahead[half:], axis, -1))
    return found


def join_kernel(*refs):
    out = refs[-1]
    offset = 0
    for piece in refs[:-1]:
        length = piece.shape[0]
        out[pl.ds(offset, length), :] = piece[...]
        offset += length


def join(blocks):
    pieces = [part for block in blocks for part in block]
    total = sum(piece.shape[0] for piece in pieces)
    vmem = pl.BlockSpec(memory_space=pltpu.VMEM)
    return pl.pallas_call(
        join_kernel,
        out_shape=jax.ShapeDtypeStruct((total, WIDTH), jnp.float32),
        in_specs=[vmem] * len(pieces),
        out_specs=vmem,
        compiler_params=pltpu.CompilerParams(vmem_limit_bytes=LIMIT * 1024 * 1024),
        cost_estimate=pl.CostEstimate(flops=0, bytes_accessed=total * WIDTH * 8, transcendentals=0),
        name="join",
    )(*pieces)


def plan_kernel(fill, kind, *refs):
    plan, counts = refs[:3], refs[3]

    def list_bucket(b, ends):
        def put(j, ends):
            slot = b * PER_BUCKET + j
            which = kind[slot]
            for k in range(3):
                plan[k][ends[k]] = slot
            return tuple(e + (which == k).astype(jnp.int32) for k, e in enumerate(ends))

        return lax.fori_loop(0, fill[b], put, ends)

    ends = lax.fori_loop(0, BUCKETS, list_bucket, (0, 0, 0))
    for k in range(3):
        counts[k] = ends[k]


def slot_plan(fill, kind):
    smem = pl.BlockSpec(memory_space=pltpu.SMEM)
    return pl.pallas_call(
        plan_kernel,
        out_shape=[jax.ShapeDtypeStruct((SLOTS,), jnp.int32)] * 3
        + [jax.ShapeDtypeStruct((3,), jnp.int32)],
        in_specs=[smem, smem],
        out_specs=[smem] * 4,
        cost_estimate=pl.CostEstimate(flops=0, bytes_accessed=12 * 1024 * 1024, transcendentals=0),
        name="slot_plan",
    )(fill, kind)


def products_kernel(part, counts, listed, blk, row, tiles, panels, *refs):
    first_row = FAR_ROW if part == 1 else 0
    if part == 0:
        total, held, tile_sem = refs
    else:
        before, outs = refs[0], refs[1:-3]
        total, held, tile_sem = refs[-3:]
    count = counts[part]

    def tile_copy(i):
        return pltpu.make_async_copy(tiles.at[listed[i]], held.at[i], tile_sem.at[i])

    @pl.loop(0, count)
    def _(i):
        tile_copy(i).start()

    total[...] = before[first_row : first_row + total.shape[0]] if part else jnp.zeros_like(total)

    def product(i):
        slot = listed[i]
        tile = held[i]
        panel = panels[pl.ds(pl.multiple_of(blk[slot] * EDGE, EDGE), EDGE), :]
        tile_hi = tile.astype(jnp.bfloat16)
        tile_lo = (tile - tile_hi.astype(jnp.float32)).astype(jnp.bfloat16)
        panel_hi = panel.astype(jnp.bfloat16)
        panel_lo = (panel - panel_hi.astype(jnp.float32)).astype(jnp.bfloat16)
        left = jnp.concatenate([tile_hi, tile_hi, tile_lo], axis=1)
        right = jnp.concatenate([panel_hi, panel_lo, panel_hi], axis=0)
        return jnp.dot(left, right, preferred_element_type=jnp.float32)

    groups = count // GROUP

    @pl.loop(0, groups)
    def _(g):
        slots = [g * GROUP + n for n in range(GROUP)]
        for i in slots:
            tile_copy(i).wait()
        sums = [product(i) for i in slots]
        for i, value in zip(slots, sums):
            total[row[listed[i]] - first_row] += value

    @pl.loop(groups * GROUP, count)
    def _(i):
        tile_copy(i).wait()
        total[row[listed[i]] - first_row] += product(i)

    if part:
        offset = 0
        for out in outs:
            length = out.shape[0]
            out[...] = total[offset : offset + length]
            offset += length


def slot_products(part, tables, tiles, panels, before=None):
    any_space = pl.BlockSpec(memory_space=pl.ANY)
    smem = pl.BlockSpec(memory_space=pltpu.SMEM)
    vmem = pl.BlockSpec(memory_space=pltpu.VMEM)
    block = lambda n: jax.ShapeDtypeStruct((n, EDGE, WIDTH), jnp.float32)
    scratch = [pltpu.VMEM((SLOTS, EDGE, EDGE), jnp.float32), pltpu.SemaphoreType.DMA((SLOTS,))]
    arrays = [tiles, panels]
    if part == 0:
        shapes = [block(BLOCKS)]
    else:
        shapes = [block(4), block(4)] if part == 1 else [block(8)] + [block(4)] * 4
        rows = BLOCKS - FAR_ROW if part == 1 else FAR_ROW
        scratch = [pltpu.VMEM((rows, EDGE, WIDTH), jnp.float32)] + scratch
        arrays.append(before)
    share = (4, 1, 3)[part]
    return pl.pallas_call(
        functools.partial(products_kernel, part),
        out_shape=shapes,
        in_specs=[smem] * 4 + [any_space] + [vmem] * (len(arrays) - 1),
        out_specs=[vmem] * len(shapes),
        scratch_shapes=scratch,
        compiler_params=pltpu.CompilerParams(vmem_limit_bytes=LIMIT * 1024 * 1024),
        cost_estimate=pl.CostEstimate(
            flops=share * SLOTS * EDGE * EDGE * WIDTH,
            bytes_accessed=share * 3 * 1024 * 1024,
            transcendentals=0,
        ),
        name="slot_products",
    )(*tables, *arrays)


BAND = 64


def factor_kernel(gram, rows, embedding, factor, work):
    work[:, :WIDTH] = gram[...]
    work[:, WIDTH:] = rows[...].T
    lane = lax.broadcasted_iota(jnp.int32, (8, EDGE), 1)
    sub = lax.broadcasted_iota(jnp.int32, (8, EDGE), 0)
    columns = (WIDTH + EDGE) // EDGE

    def along_lanes(value, at):
        return jnp.broadcast_to(value[:, at : at + 1], (8, EDGE))

    def along_rows(value, at):
        return jnp.broadcast_to(value[at : at + 1, :], (8, EDGE))

    for band in range(WIDTH // BAND):
        top = band * BAND
        lead = top // EDGE
        strips = BAND // 8
        held = [
            [work[top + 8 * s : top + 8 * s + 8, c * EDGE : (c + 1) * EDGE] for c in range(lead, columns)]
            for s in range(strips)
        ]
        for s0 in range(strips):
            at = (top + 8 * s0) % EDGE
            cols = {s: [along_lanes(held[s][0], at + q) for q in range(8)] for s in range(s0, strips)}
            block = {(t, r): along_rows(cols[s0][r], t) for t in range(8) for r in range(t + 1)}
            lower = {}
            inverse = []
            root = []
            for q in range(8):
                inverse.append(1.0 / block[q, q])
                root.append(lax.rsqrt(block[q, q]))
                for t in range(q + 1, 8):
                    lower[t, q] = block[t, q] * inverse[q]
                for t in range(q + 1, 8):
                    for r in range(q + 1, t + 1):
                        block[t, r] = block[t, r] - lower[t, q] * block[r, q]
            lines = []
            for q in range(8):
                line = [along_rows(v, q) for v in held[s0]]
                for t in range(q):
                    line = [v - lower[q, t] * w for v, w in zip(line, lines[t])]
                lines.append(line)
            for s in range(s0 + 1, strips):
                weights = []
                for q in range(8):
                    value = cols[s][q]
                    for t in range(q):
                        value = value - lower[q, t] * weights[t]
                    weights.append(value)
                weights = [v * w for v, w in zip(weights, inverse)]
                for q in range(8):
                    held[s] = [v - weights[q] * w for v, w in zip(held[s], lines[q])]
            final = [jnp.zeros((8, EDGE), jnp.float32)] * len(held[s0])
            for q in range(8):
                final = [jnp.where(sub == q, w * root[q], v) for v, w in zip(final, lines[q])]
            for c in range(lead, columns):
                value = final[c - lead]
                if c < WIDTH // EDGE:
                    value = jnp.where(lane + c * EDGE >= sub + (top + 8 * s0), value, 0.0)
                work[top + 8 * s0 : top + 8 * s0 + 8, c * EDGE : (c + 1) * EDGE] = value
        below = top + BAND
        if below < WIDTH:
            base = below // EDGE * EDGE
            left = work[top:below, base:WIDTH]
            right = work[top:below, base:]
            update = lax.dot_general(
                left,
                right,
                (((0,), (0,)), ((), ())),
                precision=lax.Precision.HIGHEST,
                preferred_element_type=jnp.float32,
            )
            work[below:, base:] -= update[below - base :, :]
    scale = jnp.sqrt(jnp.float32(ROWS))
    for band in range(WIDTH // BAND):
        top = band * BAND
        lead = top // EDGE * EDGE
        if lead:
            factor[top : top + BAND, :lead] = jnp.zeros((BAND, lead), jnp.float32)
        factor[top : top + BAND, lead:] = work[top : top + BAND, lead:WIDTH] / scale
    embedding[...] = work[:, WIDTH:].T * scale


def factor_and_solve(gram, rows):
    vmem = pl.BlockSpec(memory_space=pltpu.VMEM)
    return pl.pallas_call(
        factor_kernel,
        out_shape=[
            jax.ShapeDtypeStruct((EDGE, WIDTH), jnp.float32),
            jax.ShapeDtypeStruct((WIDTH, WIDTH), jnp.float32),
        ],
        in_specs=[vmem, vmem],
        out_specs=[vmem, vmem],
        scratch_shapes=[pltpu.VMEM((WIDTH, WIDTH + EDGE), jnp.float32)],
        compiler_params=pltpu.CompilerParams(vmem_limit_bytes=16 * 1024 * 1024),
        name="factor_and_solve",
    )(gram, rows)


def exchange(value, axes):
    return lax.all_to_all(value, axes, 0, 0, tiled=True)


def on_device(tiles, tile_rows, tile_cols, bucket_fill, row_slot, sketch):
    here_x = lax.axis_index("x")
    here_z = lax.axis_index("z")
    here_core = lax.axis_index("core")

    slot_ids = jnp.arange(SLOTS, dtype=jnp.int32)
    bucket = slot_ids // PER_BUCKET
    cols = tile_cols[0, 0]
    far_x = (bucket // 8 - here_x) % 4
    far_z = (bucket % 8 - here_z) % 8
    blk = jnp.where(cols % 2 == 0, far_z * 4 + far_x, 32 + far_x * 8 + far_z)
    side = (cols // 2 + here_core) % 2
    block_ids = jnp.arange(BLOCKS, dtype=jnp.int32)
    target = jnp.sum(
        jnp.where(tile_rows[0, 0][:, None] == block_ids[None, :], row_slot[0][None, :], 0), axis=1
    )
    ahead = (target // 8 - here_x) % 4
    chunk = jnp.where(ahead == 3, 2, jnp.where(ahead == 2, 3, ahead))
    row = chunk * 8 + (target % 8 - here_z) % 8
    kind = jnp.where(side == 0, 0, jnp.where(row >= FAR_ROW, 1, 2))

    with jax.named_scope("gather"):
        mine = lax.dynamic_slice_in_dim(sketch, here_core * 2 * EDGE, 2 * EDGE, 0)
        slab = join(ring_gather(mine[:EDGE], "x", True))
        line = join(ring_gather(mine[EDGE:], "z", True))
        first = ring_gather(slab, "z")
        second = ring_gather(line, "x")
        slab, *plan, counts = lax.optimization_barrier((slab, *slot_plan(bucket_fill[0, 0], kind)))
        panels = join([(slab,)] + first[1:] + second)
        panels_other = shift(panels, "core", 1)

    stack = tiles[0, 0]
    tables = [(counts, listed, blk, row) for listed in plan]
    (sums,) = slot_products(0, tables[0], stack, panels)
    far = slot_products(1, tables[1], stack, panels_other, sums)
    near = slot_products(2, tables[2], stack, panels_other, sums)

    with jax.named_scope("scatter_rows"):
        far_below, far_above = shift(far[0], "x", 1), shift(far[1], "x", -1)
        own, up_low, up_high, down_low, down_high = near
        up_low = up_low + far_below
        down_high = down_high + far_above
        high_below, low_above = shift(up_high, "x", 1), shift(down_low, "x", -1)
        low_below, high_above = shift(up_low, "x", 1), shift(down_high, "x", -1)
        own = jnp.concatenate(
            [own[:4] + low_below + low_above, own[4:] + high_below + high_above], axis=0
        )
        half = EDGE // 2
        from_below, from_above = both_ways(own[4, :half], own[4, half:], "z")
        up = jnp.stack([own[2], join_rows(own[3, :half] + from_below, own[3, half:])])
        down = jnp.stack([own[6], join_rows(own[5, :half], own[5, half:] + from_above)])
        from_below, from_above = both_ways(up, down, "z", 2)
        up = own[1] + from_below[1]
        down = own[7] + from_above[1]
        middle = own[0] + from_below[0] + from_above[0]
        from_below, from_above = both_ways(up, down, "z")
        product_rows = middle + from_below + from_above

    with jax.named_scope("gram"):
        gram = jnp.dot(
            product_rows.T,
            product_rows,
            precision=lax.Precision.HIGHEST,
            preferred_element_type=jnp.float32,
        )
        ring = ("y", "core", "x")
        part = jnp.sum(exchange(gram, ring).reshape(32, 8, WIDTH), axis=0)
        part = jnp.sum(
            exchange(jnp.broadcast_to(part[None], (8, 8, WIDTH)), "z"), axis=0
        )
        gram = exchange(jnp.broadcast_to(part[None], (32, 8, WIDTH)), ring).reshape(WIDTH, WIDTH)

    embedding, factor = factor_and_solve(gram, product_rows)
    return embedding, factor


def solution(mesh):
    fine = Mesh(mesh.devices.reshape(SIZES), AXES)
    grp, col = ("y", "core"), ("x", "z")
    placed = (
        P(grp, col, None, None, None),
        P(grp, col, None),
        P(grp, col, None),
        P(grp, col, None),
        P(grp, None),
        P(col, None),
    )
    return jax.shard_map(
        on_device,
        mesh=fine,
        in_specs=placed,
        out_specs=(P(AXES, None), P()),
        check_vma=False,
    )
```

```python
import functools

import jax
import jax.numpy as jnp
from jax import lax
from jax.experimental import pallas as pl
from jax.experimental.pallas import tpu as pltpu
from jax.sharding import Mesh
from jax.sharding import PartitionSpec as P

AXES = ("y", "core", "x", "z")
SIZES = (4, 2, 4, 8)
EDGE = 128
WIDTH = 256
BLOCKS = 32
BUCKETS = 32
PER_BUCKET = 6
SLOTS = 192
ROWS = 32768
GROUP = 8
HELD = 96
LIMIT = 30
FAR_ROW = 24


def shift(value, axis, step):
    count = lax.axis_size(axis)
    return lax.ppermute(value, axis, [(i, (i + step) % count) for i in range(count)])


def both_ways(up, down, axis, step=1):
    up, down = lax.optimization_barrier((up, down))
    return lax.optimization_barrier((shift(up, axis, step), shift(down, axis, -step)))


def join_rows(top, bottom):
    return jnp.concatenate([top, bottom], axis=0)


def ring_gather(block, axis, by_core=False):
    count = lax.axis_size(axis)
    found = [None] * count
    found[0] = (block,)
    behind = ahead = block
    for step in range(1, count // 2):
        behind = shift(behind, axis, 1)
        ahead = shift(ahead, axis, -1)
        found[count - step] = (behind,)
        found[step] = (ahead,)
    if by_core:
        pairs = [
            (core * count + i, core * count + (i + 1 - 2 * core) % count)
            for core in range(2)
            for i in range(count)
        ]
        value = jnp.where(lax.axis_index("core") == 0, behind, ahead)
        found[count // 2] = (lax.ppermute(value, ("core", axis), pairs),)
    else:
        half = block.shape[0] // 2
        found[count // 2] = (shift(behind[:half], axis, 1), shift(ahead[half:], axis, -1))
    return found


def join_kernel(*refs):
    out = refs[-1]
    offset = 0
    for piece in refs[:-1]:
        length = piece.shape[0]
        out[pl.ds(offset, length), :] = piece[...]
        offset += length


def join(blocks):
    pieces = [part for block in blocks for part in block]
    total = sum(piece.shape[0] for piece in pieces)
    vmem = pl.BlockSpec(memory_space=pltpu.VMEM)
    return pl.pallas_call(
        join_kernel,
        out_shape=jax.ShapeDtypeStruct((total, WIDTH), jnp.float32),
        in_specs=[vmem] * len(pieces),
        out_specs=vmem,
        compiler_params=pltpu.CompilerParams(vmem_limit_bytes=8 * 1024 * 1024),
        cost_estimate=pl.CostEstimate(flops=0, bytes_accessed=total * WIDTH * 8, transcendentals=0),
        name="join",
    )(*pieces)


def place_kernel(offsets, late, *refs):
    pieces, out, sem = refs[late:-2], refs[-2], refs[-1]
    copies = [
        pltpu.make_async_copy(piece, out.at[pl.ds(offset, piece.shape[0])], sem.at[n])
        for n, (piece, offset) in enumerate(zip(pieces, offsets))
    ]
    for copy in copies:
        copy.start()
    for copy in copies:
        copy.wait()


def place(pieces, total, before=None):
    late = before is not None
    vmem = pl.BlockSpec(memory_space=pltpu.VMEM)
    any_space = pl.BlockSpec(memory_space=pl.ANY)
    offsets, arrays = zip(*pieces)
    moved = sum(array.size for array in arrays) * 8
    return pl.pallas_call(
        functools.partial(place_kernel, offsets, int(late)),
        out_shape=jax.ShapeDtypeStruct((total, WIDTH), jnp.float32),
        in_specs=[any_space] * late + [vmem] * len(arrays),
        out_specs=any_space,
        input_output_aliases={0: 0} if late else {},
        scratch_shapes=[pltpu.SemaphoreType.DMA((len(arrays),))],
        compiler_params=pltpu.CompilerParams(vmem_limit_bytes=16 * 1024 * 1024),
        cost_estimate=pl.CostEstimate(flops=0, bytes_accessed=moved, transcendentals=0),
        name="place",
    )(*([before] if late else []), *arrays)


def plan_kernel(fill, kind, *refs):
    plan, counts = refs[:3], refs[3]

    def list_bucket(b, ends):
        def put(j, ends):
            slot = b * PER_BUCKET + j
            which = kind[slot]
            for k in range(3):
                plan[k][ends[k]] = slot
            return tuple(e + (which == k).astype(jnp.int32) for k, e in enumerate(ends))

        return lax.fori_loop(0, fill[b], put, ends)

    ends = lax.fori_loop(0, BUCKETS, list_bucket, (0, 0, 0))
    for k in range(3):
        counts[k] = ends[k]


def slot_plan(fill, kind):
    smem = pl.BlockSpec(memory_space=pltpu.SMEM)
    return pl.pallas_call(
        plan_kernel,
        out_shape=[jax.ShapeDtypeStruct((SLOTS,), jnp.int32)] * 3
        + [jax.ShapeDtypeStruct((3,), jnp.int32)],
        in_specs=[smem, smem],
        out_specs=[smem] * 4,
        cost_estimate=pl.CostEstimate(flops=0, bytes_accessed=12 * 1024 * 1024, transcendentals=0),
        name="slot_plan",
    )(fill, kind)


def products_kernel(part, counts, listed, blk, row, tiles, panels, *refs):
    first_row = FAR_ROW if part == 1 else 0
    if part == 0:
        total, held, tile_sem = refs
    else:
        before, outs = refs[0], refs[1:-3]
        total, held, tile_sem = refs[-3:]
    count = counts[part]

    def tile_copy(i):
        spot = lax.rem(i, HELD)
        return pltpu.make_async_copy(tiles.at[listed[i]], held.at[spot], tile_sem.at[spot])

    def fetch(load):
        @pl.loop(load * HELD, jnp.minimum((load + 1) * HELD, count))
        def _(i):
            tile_copy(i).start()

    fetch(0)
    total[...] = before[first_row : first_row + total.shape[0]] if part else jnp.zeros_like(total)

    def product(i):
        slot = listed[i]
        tile = held[lax.rem(i, HELD)]
        panel = panels[pl.ds(pl.multiple_of(blk[slot] * EDGE, EDGE), EDGE), :]
        tile_hi = tile.astype(jnp.bfloat16)
        tile_lo = (tile - tile_hi.astype(jnp.float32)).astype(jnp.bfloat16)
        panel_hi = panel.astype(jnp.bfloat16)
        panel_lo = (panel - panel_hi.astype(jnp.float32)).astype(jnp.bfloat16)
        left = jnp.concatenate([tile_hi, tile_hi, tile_lo], axis=1)
        right = jnp.concatenate([panel_hi, panel_lo, panel_hi], axis=0)
        return jnp.dot(left, right, preferred_element_type=jnp.float32)

    @pl.loop(0, pl.cdiv(count, HELD))
    def _(load):
        first = load * HELD
        last = jnp.minimum(first + HELD, count)
        groups = (last - first) // GROUP

        @pl.loop(0, groups)
        def _(g):
            slots = [first + g * GROUP + n for n in range(GROUP)]
            for i in slots:
                tile_copy(i).wait()
            sums = [product(i) for i in slots]
            for i, value in zip(slots, sums):
                total[row[listed[i]] - first_row] += value

        @pl.loop(first + groups * GROUP, last)
        def _(i):
            tile_copy(i).wait()
            total[row[listed[i]] - first_row] += product(i)

        fetch(load + 1)

    if part:
        offset = 0
        for out in outs:
            length = out.shape[0]
            out[...] = total[offset : offset + length]
            offset += length


def slot_products(part, tables, tiles, panels, before=None):
    any_space = pl.BlockSpec(memory_space=pl.ANY)
    smem = pl.BlockSpec(memory_space=pltpu.SMEM)
    vmem = pl.BlockSpec(memory_space=pltpu.VMEM)
    block = lambda n: jax.ShapeDtypeStruct((n, EDGE, WIDTH), jnp.float32)
    scratch = [pltpu.VMEM((HELD, EDGE, EDGE), jnp.float32), pltpu.SemaphoreType.DMA((HELD,))]
    arrays = [tiles, panels]
    if part == 0:
        shapes = [block(BLOCKS)]
    else:
        shapes = [block(4), block(4)] if part == 1 else [block(8)] + [block(4)] * 4
        rows = BLOCKS - FAR_ROW if part == 1 else FAR_ROW
        scratch = [pltpu.VMEM((rows, EDGE, WIDTH), jnp.float32)] + scratch
        arrays.append(before)
    share = (4, 1, 3)[part]
    return pl.pallas_call(
        functools.partial(products_kernel, part),
        out_shape=shapes,
        in_specs=[smem] * 4 + [any_space] + [vmem] * (len(arrays) - 1),
        out_specs=[vmem] * len(shapes),
        scratch_shapes=scratch,
        compiler_params=pltpu.CompilerParams(vmem_limit_bytes=LIMIT * 1024 * 1024),
        cost_estimate=pl.CostEstimate(
            flops=share * SLOTS * EDGE * EDGE * WIDTH,
            bytes_accessed=share * 3 * 1024 * 1024,
            transcendentals=0,
        ),
        name="slot_products",
    )(*tables, *arrays)


BAND = 64


def factor_kernel(gram, rows, embedding, factor, work):
    work[:, :WIDTH] = gram[...]
    work[:, WIDTH:] = rows[...].T
    lane = lax.broadcasted_iota(jnp.int32, (8, EDGE), 1)
    sub = lax.broadcasted_iota(jnp.int32, (8, EDGE), 0)
    columns = (WIDTH + EDGE) // EDGE

    def along_lanes(value, at):
        return jnp.broadcast_to(value[:, at : at + 1], (8, EDGE))

    def along_rows(value, at):
        return jnp.broadcast_to(value[at : at + 1, :], (8, EDGE))

    for band in range(WIDTH // BAND):
        top = band * BAND
        lead = top // EDGE
        strips = BAND // 8
        held = [
            [work[top + 8 * s : top + 8 * s + 8, c * EDGE : (c + 1) * EDGE] for c in range(lead, columns)]
            for s in range(strips)
        ]
        for s0 in range(strips):
            at = (top + 8 * s0) % EDGE
            cols = {s: [along_lanes(held[s][0], at + q) for q in range(8)] for s in range(s0, strips)}
            block = {(t, r): along_rows(cols[s0][r], t) for t in range(8) for r in range(t + 1)}
            lower = {}
            inverse = []
            root = []
            for q in range(8):
                inverse.append(1.0 / block[q, q])
                root.append(lax.rsqrt(block[q, q]))
                for t in range(q + 1, 8):
                    lower[t, q] = block[t, q] * inverse[q]
                for t in range(q + 1, 8):
                    for r in range(q + 1, t + 1):
                        block[t, r] = block[t, r] - lower[t, q] * block[r, q]
            lines = []
            for q in range(8):
                line = [along_rows(v, q) for v in held[s0]]
                for t in range(q):
                    line = [v - lower[q, t] * w for v, w in zip(line, lines[t])]
                lines.append(line)
            for s in range(s0 + 1, strips):
                weights = []
                for q in range(8):
                    value = cols[s][q]
                    for t in range(q):
                        value = value - lower[q, t] * weights[t]
                    weights.append(value)
                weights = [v * w for v, w in zip(weights, inverse)]
                for q in range(8):
                    held[s] = [v - weights[q] * w for v, w in zip(held[s], lines[q])]
            final = [jnp.zeros((8, EDGE), jnp.float32)] * len(held[s0])
            for q in range(8):
                final = [jnp.where(sub == q, w * root[q], v) for v, w in zip(final, lines[q])]
            for c in range(lead, columns):
                value = final[c - lead]
                if c < WIDTH // EDGE:
                    value = jnp.where(lane + c * EDGE >= sub + (top + 8 * s0), value, 0.0)
                work[top + 8 * s0 : top + 8 * s0 + 8, c * EDGE : (c + 1) * EDGE] = value
        below = top + BAND
        if below < WIDTH:
            base = below // EDGE * EDGE
            left = work[top:below, base:WIDTH]
            right = work[top:below, base:]
            update = lax.dot_general(
                left,
                right,
                (((0,), (0,)), ((), ())),
                precision=lax.Precision.HIGHEST,
                preferred_element_type=jnp.float32,
            )
            work[below:, base:] -= update[below - base :, :]
    scale = jnp.sqrt(jnp.float32(ROWS))
    for band in range(WIDTH // BAND):
        top = band * BAND
        lead = top // EDGE * EDGE
        if lead:
            factor[top : top + BAND, :lead] = jnp.zeros((BAND, lead), jnp.float32)
        factor[top : top + BAND, lead:] = work[top : top + BAND, lead:WIDTH] / scale
    embedding[...] = work[:, WIDTH:].T * scale


def factor_and_solve(gram, rows):
    vmem = pl.BlockSpec(memory_space=pltpu.VMEM)
    return pl.pallas_call(
        factor_kernel,
        out_shape=[
            jax.ShapeDtypeStruct((EDGE, WIDTH), jnp.float32),
            jax.ShapeDtypeStruct((WIDTH, WIDTH), jnp.float32),
        ],
        in_specs=[vmem, vmem],
        out_specs=[vmem, vmem],
        scratch_shapes=[pltpu.VMEM((WIDTH, WIDTH + EDGE), jnp.float32)],
        compiler_params=pltpu.CompilerParams(vmem_limit_bytes=16 * 1024 * 1024),
        name="factor_and_solve",
    )(gram, rows)


def exchange(value, axes):
    return lax.all_to_all(value, axes, 0, 0, tiled=True)


def on_device(tiles, tile_rows, tile_cols, bucket_fill, row_slot, sketch):
    here_x = lax.axis_index("x")
    here_z = lax.axis_index("z")
    here_core = lax.axis_index("core")

    slot_ids = jnp.arange(SLOTS, dtype=jnp.int32)
    bucket = slot_ids // PER_BUCKET
    cols = tile_cols[0, 0]
    far_x = (bucket // 8 - here_x) % 4
    far_z = (bucket % 8 - here_z) % 8
    blk = jnp.where(cols % 2 == 0, far_z * 4 + far_x, 32 + far_x * 8 + far_z)
    side = (cols // 2 + here_core) % 2
    block_ids = jnp.arange(BLOCKS, dtype=jnp.int32)
    target = jnp.sum(
        jnp.where(tile_rows[0, 0][:, None] == block_ids[None, :], row_slot[0][None, :], 0), axis=1
    )
    ahead = (target // 8 - here_x) % 4
    chunk = jnp.where(ahead == 3, 2, jnp.where(ahead == 2, 3, ahead))
    row = chunk * 8 + (target % 8 - here_z) % 8
    kind = jnp.where(side == 0, 0, jnp.where(row >= FAR_ROW, 1, 2))

    with jax.named_scope("gather"):
        mine = lax.dynamic_slice_in_dim(sketch, here_core * 2 * EDGE, 2 * EDGE, 0)
        slab = join(ring_gather(mine[:EDGE], "x", True))
        line = join(ring_gather(mine[EDGE:], "z", True))
        first = ring_gather(slab, "z")
        second = ring_gather(line, "x")
        slab, *plan, counts = lax.optimization_barrier((slab, *slot_plan(bucket_fill[0, 0], kind)))
        first[0] = (slab,)
        early, final = [], []
        for base, found in ((0, first), (first[0][0].shape[0] * len(first), second)):
            length = found[0][0].shape[0]
            for distance, parts in enumerate(found):
                group = final if len(parts) > 1 else early
                for n, part in enumerate(parts):
                    group.append((base + distance * length + n * part.shape[0], part))
        total = BLOCKS * 2 * EDGE
        panels = place(final, total, place(early, total))
        panels_other = shift(panels, "core", 1)

    stack = tiles[0, 0]
    tables = [(counts, listed, blk, row) for listed in plan]
    (sums,) = slot_products(0, tables[0], stack, panels)
    far = slot_products(1, tables[1], stack, panels_other, sums)
    near = slot_products(2, tables[2], stack, panels_other, sums)

    with jax.named_scope("scatter_rows"):
        far_below, far_above = shift(far[0], "x", 1), shift(far[1], "x", -1)
        own, up_low, up_high, down_low, down_high = near
        up_low = up_low + far_below
        down_high = down_high + far_above
        high_below, low_above = shift(up_high, "x", 1), shift(down_low, "x", -1)
        low_below, high_above = shift(up_low, "x", 1), shift(down_high, "x", -1)
        own = jnp.concatenate(
            [own[:4] + low_below + low_above, own[4:] + high_below + high_above], axis=0
        )
        half = EDGE // 2
        from_below, from_above = both_ways(own[4, :half], own[4, half:], "z")
        up = jnp.stack([own[2], join_rows(own[3, :half] + from_below, own[3, half:])])
        down = jnp.stack([own[6], join_rows(own[5, :half], own[5, half:] + from_above)])
        from_below, from_above = both_ways(up, down, "z", 2)
        up = own[1] + from_below[1]
        down = own[7] + from_above[1]
        middle = own[0] + from_below[0] + from_above[0]
        from_below, from_above = both_ways(up, down, "z")
        product_rows = middle + from_below + from_above

    with jax.named_scope("gram"):
        gram = jnp.dot(
            product_rows.T,
            product_rows,
            precision=lax.Precision.HIGHEST,
            preferred_element_type=jnp.float32,
        )
        ring = ("y", "core", "x")
        part = jnp.sum(exchange(gram, ring).reshape(32, 8, WIDTH), axis=0)
        part = jnp.sum(
            exchange(jnp.broadcast_to(part[None], (8, 8, WIDTH)), "z"), axis=0
        )
        gram = exchange(jnp.broadcast_to(part[None], (32, 8, WIDTH)), ring).reshape(WIDTH, WIDTH)

    embedding, factor = factor_and_solve(gram, product_rows)
    return embedding, factor


def solution(mesh):
    fine = Mesh(mesh.devices.reshape(SIZES), AXES)
    grp, col = ("y", "core"), ("x", "z")
    placed = (
        P(grp, col, None, None, None),
        P(grp, col, None),
        P(grp, col, None),
        P(grp, col, None),
        P(grp, None),
        P(col, None),
    )
    return jax.shard_map(
        on_device,
        mesh=fine,
        in_specs=placed,
        out_specs=(P(AXES, None), P()),
        check_vma=False,
    )
```

```python
import functools

import jax
import jax.numpy as jnp
from jax import lax
from jax.experimental import pallas as pl
from jax.experimental.pallas import tpu as pltpu
from jax.sharding import Mesh
from jax.sharding import PartitionSpec as P

AXES = ("y", "core", "x", "z")
SIZES = (4, 2, 4, 8)
EDGE = 128
WIDTH = 256
BLOCKS = 32
BUCKETS = 32
PER_BUCKET = 6
SLOTS = 192
ROWS = 32768
GROUP = 8
HELD = 96
LIMIT = 30
FAR_ROW = 24


def shift(value, axis, step):
    count = lax.axis_size(axis)
    pairs = [
        (core * count + i, core * count + (i + step - 2 * core * step) % count)
        for core in range(2)
        for i in range(count)
    ]
    return lax.ppermute(value, ("core", axis), pairs)


def swap(value):
    return lax.ppermute(value, "core", [(0, 1), (1, 0)])


def ring_gather(block, axis):
    count = lax.axis_size(axis)
    found = [None] * count
    found[0] = behind = ahead = block
    for step in range(1, count // 2):
        behind = shift(behind, axis, 1)
        ahead = shift(ahead, axis, -1)
        found[count - step] = behind
        found[step] = ahead
    found[count // 2] = shift(behind, axis, 1)
    return found


def join_kernel(*refs):
    out = refs[-1]
    offset = 0
    for piece in refs[:-1]:
        length = piece.shape[0]
        out[pl.ds(offset, length), :] = piece[...]
        offset += length


def join(pieces):
    total = sum(piece.shape[0] for piece in pieces)
    vmem = pl.BlockSpec(memory_space=pltpu.VMEM)
    return pl.pallas_call(
        join_kernel,
        out_shape=jax.ShapeDtypeStruct((total, WIDTH), jnp.float32),
        in_specs=[vmem] * len(pieces),
        out_specs=vmem,
        compiler_params=pltpu.CompilerParams(vmem_limit_bytes=8 * 1024 * 1024),
        cost_estimate=pl.CostEstimate(flops=0, bytes_accessed=total * WIDTH * 8, transcendentals=0),
        name="join",
    )(*pieces)


def place_kernel(offsets, late, *refs):
    pieces, out, sem = refs[late:-2], refs[-2], refs[-1]
    copies = [
        pltpu.make_async_copy(piece, out.at[pl.ds(offset, piece.shape[0])], sem.at[n])
        for n, (piece, offset) in enumerate(zip(pieces, offsets))
    ]
    for copy in copies:
        copy.start()
    for copy in copies:
        copy.wait()


def place(pieces, total, before=None):
    late = before is not None
    vmem = pl.BlockSpec(memory_space=pltpu.VMEM)
    any_space = pl.BlockSpec(memory_space=pl.ANY)
    offsets, arrays = zip(*pieces)
    moved = sum(array.size for array in arrays) * 8
    return pl.pallas_call(
        functools.partial(place_kernel, offsets, int(late)),
        out_shape=jax.ShapeDtypeStruct((total, WIDTH), jnp.float32),
        in_specs=[any_space] * late + [vmem] * len(arrays),
        out_specs=any_space,
        input_output_aliases={0: 0} if late else {},
        scratch_shapes=[pltpu.SemaphoreType.DMA((len(arrays),))],
        compiler_params=pltpu.CompilerParams(vmem_limit_bytes=16 * 1024 * 1024),
        cost_estimate=pl.CostEstimate(flops=0, bytes_accessed=moved, transcendentals=0),
        name="place",
    )(*([before] if late else []), *arrays)


def plan_kernel(fill, kind, *refs):
    plan, counts = refs[:3], refs[3]

    def list_bucket(b, ends):
        def put(j, ends):
            slot = b * PER_BUCKET + j
            which = kind[slot]
            for k in range(3):
                plan[k][ends[k]] = slot
            return tuple(e + (which == k).astype(jnp.int32) for k, e in enumerate(ends))

        return lax.fori_loop(0, fill[b], put, ends)

    ends = lax.fori_loop(0, BUCKETS, list_bucket, (0, 0, 0))
    for k in range(3):
        counts[k] = ends[k]


def slot_plan(fill, kind):
    smem = pl.BlockSpec(memory_space=pltpu.SMEM)
    return pl.pallas_call(
        plan_kernel,
        out_shape=[jax.ShapeDtypeStruct((SLOTS,), jnp.int32)] * 3
        + [jax.ShapeDtypeStruct((3,), jnp.int32)],
        in_specs=[smem, smem],
        out_specs=[smem] * 4,
        compiler_params=pltpu.CompilerParams(vmem_limit_bytes=1024 * 1024),
        cost_estimate=pl.CostEstimate(flops=0, bytes_accessed=12 * 1024 * 1024, transcendentals=0),
        name="slot_plan",
    )(fill, kind)


def products_kernel(part, counts, listed, blk, row, tiles, panels, *refs):
    first_row = FAR_ROW if part == 1 else 0
    if part == 0:
        total, held, tile_sem = refs
    else:
        before, outs = refs[0], refs[1:-3]
        total, held, tile_sem = refs[-3:]
    count = counts[part]

    def tile_copy(i):
        spot = lax.rem(i, HELD)
        return pltpu.make_async_copy(tiles.at[listed[i]], held.at[spot], tile_sem.at[spot])

    def fetch(load):
        @pl.loop(load * HELD, jnp.minimum((load + 1) * HELD, count))
        def _(i):
            tile_copy(i).start()

    fetch(0)
    total[...] = before[first_row : first_row + total.shape[0]] if part else jnp.zeros_like(total)

    def product(i):
        slot = listed[i]
        tile = held[lax.rem(i, HELD)]
        panel = panels[pl.ds(pl.multiple_of(blk[slot] * EDGE, EDGE), EDGE), :]
        tile_hi = tile.astype(jnp.bfloat16)
        tile_lo = (tile - tile_hi.astype(jnp.float32)).astype(jnp.bfloat16)
        panel_hi = panel.astype(jnp.bfloat16)
        panel_lo = (panel - panel_hi.astype(jnp.float32)).astype(jnp.bfloat16)
        left = jnp.concatenate([tile_hi, tile_hi, tile_lo], axis=1)
        right = jnp.concatenate([panel_hi, panel_lo, panel_hi], axis=0)
        return jnp.dot(left, right, preferred_element_type=jnp.float32)

    @pl.loop(0, pl.cdiv(count, HELD))
    def _(load):
        first = load * HELD
        last = jnp.minimum(first + HELD, count)
        groups = (last - first) // GROUP

        @pl.loop(0, groups)
        def _(g):
            slots = [first + g * GROUP + n for n in range(GROUP)]
            for i in slots:
                tile_copy(i).wait()
            sums = [product(i) for i in slots]
            for i, value in zip(slots, sums):
                total[row[listed[i]] - first_row] += value

        @pl.loop(first + groups * GROUP, last)
        def _(i):
            tile_copy(i).wait()
            total[row[listed[i]] - first_row] += product(i)

        fetch(load + 1)

    if part:
        offset = 0
        for out in outs:
            length = out.shape[0]
            out[...] = total[offset : offset + length]
            offset += length


def slot_products(part, tables, tiles, panels, before=None):
    any_space = pl.BlockSpec(memory_space=pl.ANY)
    smem = pl.BlockSpec(memory_space=pltpu.SMEM)
    vmem = pl.BlockSpec(memory_space=pltpu.VMEM)
    block = lambda n: jax.ShapeDtypeStruct((n, EDGE, WIDTH), jnp.float32)
    scratch = [pltpu.VMEM((HELD, EDGE, EDGE), jnp.float32), pltpu.SemaphoreType.DMA((HELD,))]
    arrays = [tiles, panels]
    if part == 0:
        shapes = [block(BLOCKS)]
    else:
        shapes = [block(8)] if part == 1 else [block(8)] * 3
        rows = BLOCKS - FAR_ROW if part == 1 else FAR_ROW
        scratch = [pltpu.VMEM((rows, EDGE, WIDTH), jnp.float32)] + scratch
        arrays.append(before)
    share = (4, 1, 3)[part]
    return pl.pallas_call(
        functools.partial(products_kernel, part),
        out_shape=shapes,
        in_specs=[smem] * 4 + [any_space] + [vmem] * (len(arrays) - 1),
        out_specs=[vmem] * len(shapes),
        scratch_shapes=scratch,
        compiler_params=pltpu.CompilerParams(vmem_limit_bytes=LIMIT * 1024 * 1024),
        cost_estimate=pl.CostEstimate(
            flops=share * SLOTS * EDGE * EDGE * WIDTH,
            bytes_accessed=share * 3 * 1024 * 1024,
            transcendentals=0,
        ),
        name="slot_products",
    )(*tables, *arrays)


BAND = 64


def factor_kernel(gram, rows, embedding, factor, work):
    work[:, :WIDTH] = gram[...]
    work[:, WIDTH:] = rows[...].T
    lane = lax.broadcasted_iota(jnp.int32, (8, EDGE), 1)
    sub = lax.broadcasted_iota(jnp.int32, (8, EDGE), 0)
    columns = (WIDTH + EDGE) // EDGE

    def along_lanes(value, at):
        return jnp.broadcast_to(value[:, at : at + 1], (8, EDGE))

    def along_rows(value, at):
        return jnp.broadcast_to(value[at : at + 1, :], (8, EDGE))

    for band in range(WIDTH // BAND):
        top = band * BAND
        lead = top // EDGE
        strips = BAND // 8
        held = [
            [work[top + 8 * s : top + 8 * s + 8, c * EDGE : (c + 1) * EDGE] for c in range(lead, columns)]
            for s in range(strips)
        ]
        for s0 in range(strips):
            at = (top + 8 * s0) % EDGE
            cols = {s: [along_lanes(held[s][0], at + q) for q in range(8)] for s in range(s0, strips)}
            block = {(t, r): along_rows(cols[s0][r], t) for t in range(8) for r in range(t + 1)}
            lower = {}
            inverse = []
            root = []
            for q in range(8):
                inverse.append(1.0 / block[q, q])
                root.append(lax.rsqrt(block[q, q]))
                for t in range(q + 1, 8):
                    lower[t, q] = block[t, q] * inverse[q]
                for t in range(q + 1, 8):
                    for r in range(q + 1, t + 1):
                        block[t, r] = block[t, r] - lower[t, q] * block[r, q]
            lines = []
            for q in range(8):
                line = [along_rows(v, q) for v in held[s0]]
                for t in range(q):
                    line = [v - lower[q, t] * w for v, w in zip(line, lines[t])]
                lines.append(line)
            for s in range(s0 + 1, strips):
                weights = []
                for q in range(8):
                    value = cols[s][q]
                    for t in range(q):
                        value = value - lower[q, t] * weights[t]
                    weights.append(value)
                weights = [v * w for v, w in zip(weights, inverse)]
                for q in range(8):
                    held[s] = [v - weights[q] * w for v, w in zip(held[s], lines[q])]
            final = [jnp.zeros((8, EDGE), jnp.float32)] * len(held[s0])
            for q in range(8):
                final = [jnp.where(sub == q, w * root[q], v) for v, w in zip(final, lines[q])]
            for c in range(lead, columns):
                value = final[c - lead]
                if c < WIDTH // EDGE:
                    value = jnp.where(lane + c * EDGE >= sub + (top + 8 * s0), value, 0.0)
                work[top + 8 * s0 : top + 8 * s0 + 8, c * EDGE : (c + 1) * EDGE] = value
        below = top + BAND
        if below < WIDTH:
            base = below // EDGE * EDGE
            left = work[top:below, base:WIDTH]
            right = work[top:below, base:]
            update = lax.dot_general(
                left,
                right,
                (((0,), (0,)), ((), ())),
                precision=lax.Precision.HIGHEST,
                preferred_element_type=jnp.float32,
            )
            work[below:, base:] -= update[below - base :, :]
    scale = jnp.sqrt(jnp.float32(ROWS))
    for band in range(WIDTH // BAND):
        top = band * BAND
        lead = top // EDGE * EDGE
        if lead:
            factor[top : top + BAND, :lead] = jnp.zeros((BAND, lead), jnp.float32)
        factor[top : top + BAND, lead:] = work[top : top + BAND, lead:WIDTH] / scale
    embedding[...] = work[:, WIDTH:].T * scale


def factor_and_solve(gram, rows):
    vmem = pl.BlockSpec(memory_space=pltpu.VMEM)
    return pl.pallas_call(
        factor_kernel,
        out_shape=[
            jax.ShapeDtypeStruct((EDGE, WIDTH), jnp.float32),
            jax.ShapeDtypeStruct((WIDTH, WIDTH), jnp.float32),
        ],
        in_specs=[vmem, vmem],
        out_specs=[vmem, vmem],
        scratch_shapes=[pltpu.VMEM((WIDTH, WIDTH + EDGE), jnp.float32)],
        compiler_params=pltpu.CompilerParams(vmem_limit_bytes=16 * 1024 * 1024),
        name="factor_and_solve",
    )(gram, rows)


def exchange(value, axes):
    return lax.all_to_all(value, axes, 0, 0, tiled=True)


def on_device(tiles, tile_rows, tile_cols, bucket_fill, row_slot, sketch):
    here_x = lax.axis_index("x")
    here_z = lax.axis_index("z")
    here_core = lax.axis_index("core")

    slot_ids = jnp.arange(SLOTS, dtype=jnp.int32)
    bucket = slot_ids // PER_BUCKET
    cols = tile_cols[0, 0]
    side = (cols // 2 + here_core) % 2
    facing = 1 - 2 * (cols // 2)
    here_facing = 1 - 2 * here_core
    far_x = ((bucket // 8 - here_x) * facing) % 4
    far_z = ((bucket % 8 - here_z) * facing) % 8
    blk = jnp.where(cols % 2 == 0, far_z * 4 + far_x, 32 + far_x * 8 + far_z)
    block_ids = jnp.arange(BLOCKS, dtype=jnp.int32)
    target = jnp.sum(
        jnp.where(tile_rows[0, 0][:, None] == block_ids[None, :], row_slot[0][None, :], 0), axis=1
    )
    ahead = ((target // 8 - here_x) * here_facing) % 4
    chunk = jnp.where(ahead == 3, 1, jnp.where(ahead == 0, 0, ahead + 1))
    row = chunk * 8 + ((target % 8 - here_z) * here_facing) % 8
    kind = jnp.where(side == 0, 0, jnp.where(row >= FAR_ROW, 1, 2))

    with jax.named_scope("gather"):
        mine = lax.dynamic_slice_in_dim(sketch, here_core * 2 * EDGE, 2 * EDGE, 0)
        slab = join(ring_gather(mine[:EDGE], "x"))
        line = join(ring_gather(mine[EDGE:], "z"))
        first = ring_gather(slab, "z")
        second = ring_gather(line, "x")
        slab, *plan, counts = lax.optimization_barrier((slab, *slot_plan(bucket_fill[0, 0], kind)))
        first[0] = slab
        early, final = [], []
        base = 0
        for found in (first, second):
            for distance, piece in enumerate(found):
                (final if distance == len(found) // 2 else early).append((base, piece))
                base += piece.shape[0]
        panels = place(final, base, place(early, base))
        panels_other = swap(panels)

    stack = tiles[0, 0]
    tables = [(counts, listed, blk, row) for listed in plan]
    (sums,) = slot_products(0, tables[0], stack, panels)
    (far,) = slot_products(1, tables[1], stack, panels_other, sums)
    own, behind, ahead = slot_products(2, tables[2], stack, panels_other, sums)

    with jax.named_scope("scatter_rows"):
        passing = shift(far, "x", 1)
        from_ahead = shift(behind, "x", -1)
        own = own + from_ahead + shift(ahead + passing, "x", 1)
        passing = shift(own[4], "z", 1)
        ahead = jnp.stack([own[2], own[3] + passing])
        ahead, behind = lax.optimization_barrier((ahead, own[5:7]))
        ahead, behind = shift(ahead, "z", 2), shift(behind, "z", -2)
        middle = own[0] + ahead[0] + behind[1]
        ahead, behind = lax.optimization_barrier((own[1] + ahead[1], own[7] + behind[0]))
        product_rows = middle + shift(ahead, "z", 1) + shift(behind, "z", -1)

    with jax.named_scope("gram"):
        gram = jnp.dot(
            product_rows.T,
            product_rows,
            precision=lax.Precision.HIGHEST,
            preferred_element_type=jnp.float32,
        )
        ring = ("y", "core", "x")
        part = jnp.sum(exchange(gram, ring).reshape(32, 8, WIDTH), axis=0)
        part = jnp.sum(
            exchange(jnp.broadcast_to(part[None], (8, 8, WIDTH)), "z"), axis=0
        )
        gram = exchange(jnp.broadcast_to(part[None], (32, 8, WIDTH)), ring).reshape(WIDTH, WIDTH)

    embedding, factor = factor_and_solve(gram, product_rows)
    return embedding, factor


def solution(mesh):
    fine = Mesh(mesh.devices.reshape(SIZES), AXES)
    grp, col = ("y", "core"), ("x", "z")
    placed = (
        P(grp, col, None, None, None),
        P(grp, col, None),
        P(grp, col, None),
        P(grp, col, None),
        P(grp, None),
        P(col, None),
    )
    return jax.shard_map(
        on_device,
        mesh=fine,
        in_specs=placed,
        out_specs=(P(AXES, None), P()),
        check_vma=False,
    )
```

```python
import functools

import jax
import jax.numpy as jnp
from jax import lax
from jax.experimental import pallas as pl
from jax.experimental.pallas import tpu as pltpu
from jax.sharding import Mesh
from jax.sharding import PartitionSpec as P

AXES = ("y", "core", "x", "z")
SIZES = (4, 2, 4, 8)
EDGE = 128
WIDTH = 256
BLOCKS = 32
BUCKETS = 32
PER_BUCKET = 6
SLOTS = 192
ROWS = 32768
GROUP = 8
HELD = 96
LIMIT = 30
FAR_ROW = 24


def shift(value, axis, step):
    count = lax.axis_size(axis)
    pairs = [
        (core * count + i, core * count + (i + step - 2 * core * step) % count)
        for core in range(2)
        for i in range(count)
    ]
    return lax.ppermute(value, ("core", axis), pairs)


def swap(value):
    return lax.ppermute(value, "core", [(0, 1), (1, 0)])


def ring_gather(block, axis):
    count = lax.axis_size(axis)
    found = [None] * count
    found[0] = behind = ahead = block
    for step in range(1, count // 2):
        behind = shift(behind, axis, 1)
        ahead = shift(ahead, axis, -1)
        found[count - step] = behind
        found[step] = ahead
    behind, ahead = lax.optimization_barrier((behind, ahead))
    found[count // 2 + 1], found[count // 2 - 1] = behind, ahead
    found[count // 2] = shift(behind, axis, 1)
    return found


def join_kernel(*refs):
    out = refs[-1]
    offset = 0
    for piece in refs[:-1]:
        length = piece.shape[0]
        out[pl.ds(offset, length), :] = piece[...]
        offset += length


def join(pieces):
    total = sum(piece.shape[0] for piece in pieces)
    vmem = pl.BlockSpec(memory_space=pltpu.VMEM)
    return pl.pallas_call(
        join_kernel,
        out_shape=jax.ShapeDtypeStruct((total, WIDTH), jnp.float32),
        in_specs=[vmem] * len(pieces),
        out_specs=vmem,
        compiler_params=pltpu.CompilerParams(vmem_limit_bytes=8 * 1024 * 1024),
        cost_estimate=pl.CostEstimate(flops=0, bytes_accessed=total * WIDTH * 8, transcendentals=0),
        name="join",
    )(*pieces)


def place_kernel(offsets, late, *refs):
    pieces, out, sem = refs[late:-2], refs[-2], refs[-1]
    copies = [
        pltpu.make_async_copy(piece, out.at[pl.ds(offset, piece.shape[0])], sem.at[n])
        for n, (piece, offset) in enumerate(zip(pieces, offsets))
    ]
    for copy in copies:
        copy.start()
    for copy in copies:
        copy.wait()


def place(pieces, total, before=None):
    late = before is not None
    vmem = pl.BlockSpec(memory_space=pltpu.VMEM)
    any_space = pl.BlockSpec(memory_space=pl.ANY)
    offsets, arrays = zip(*pieces)
    moved = sum(array.size for array in arrays) * 8
    return pl.pallas_call(
        functools.partial(place_kernel, offsets, int(late)),
        out_shape=jax.ShapeDtypeStruct((total, WIDTH), jnp.float32),
        in_specs=[any_space] * late + [vmem] * len(arrays),
        out_specs=any_space,
        input_output_aliases={0: 0} if late else {},
        scratch_shapes=[pltpu.SemaphoreType.DMA((len(arrays),))],
        compiler_params=pltpu.CompilerParams(vmem_limit_bytes=16 * 1024 * 1024),
        cost_estimate=pl.CostEstimate(flops=0, bytes_accessed=moved, transcendentals=0),
        name="place",
    )(*([before] if late else []), *arrays)


def plan_kernel(fill, kind, *refs):
    plan, counts = refs[:3], refs[3]

    def list_bucket(b, ends):
        def put(j, ends):
            slot = b * PER_BUCKET + j
            which = kind[slot]
            for k in range(3):
                plan[k][ends[k]] = slot
            return tuple(e + (which == k).astype(jnp.int32) for k, e in enumerate(ends))

        return lax.fori_loop(0, fill[b], put, ends)

    ends = lax.fori_loop(0, BUCKETS, list_bucket, (0, 0, 0))
    for k in range(3):
        counts[k] = ends[k]


def slot_plan(fill, kind):
    smem = pl.BlockSpec(memory_space=pltpu.SMEM)
    return pl.pallas_call(
        plan_kernel,
        out_shape=[jax.ShapeDtypeStruct((SLOTS,), jnp.int32)] * 3
        + [jax.ShapeDtypeStruct((3,), jnp.int32)],
        in_specs=[smem, smem],
        out_specs=[smem] * 4,
        compiler_params=pltpu.CompilerParams(vmem_limit_bytes=1024 * 1024),
        cost_estimate=pl.CostEstimate(flops=0, bytes_accessed=12 * 1024 * 1024, transcendentals=0),
        name="slot_plan",
    )(fill, kind)


def products_kernel(part, counts, listed, blk, row, tiles, panels, *refs):
    first_row = FAR_ROW if part == 1 else 0
    if part == 0:
        total, held, tile_sem = refs
    else:
        before, outs = refs[0], refs[1:-3]
        total, held, tile_sem = refs[-3:]
    count = counts[part]

    def tile_copy(i):
        spot = lax.rem(i, HELD)
        return pltpu.make_async_copy(tiles.at[listed[i]], held.at[spot], tile_sem.at[spot])

    def fetch(load):
        @pl.loop(load * HELD, jnp.minimum((load + 1) * HELD, count))
        def _(i):
            tile_copy(i).start()

    fetch(0)
    total[...] = before[first_row : first_row + total.shape[0]] if part else jnp.zeros_like(total)

    def product(i):
        slot = listed[i]
        tile = held[lax.rem(i, HELD)]
        panel = panels[pl.ds(pl.multiple_of(blk[slot] * EDGE, EDGE), EDGE), :]
        tile_hi = tile.astype(jnp.bfloat16)
        tile_lo = (tile - tile_hi.astype(jnp.float32)).astype(jnp.bfloat16)
        panel_hi = panel.astype(jnp.bfloat16)
        panel_lo = (panel - panel_hi.astype(jnp.float32)).astype(jnp.bfloat16)
        left = jnp.concatenate([tile_hi, tile_hi, tile_lo], axis=1)
        right = jnp.concatenate([panel_hi, panel_lo, panel_hi], axis=0)
        return jnp.dot(left, right, preferred_element_type=jnp.float32)

    @pl.loop(0, pl.cdiv(count, HELD))
    def _(load):
        first = load * HELD
        last = jnp.minimum(first + HELD, count)
        groups = (last - first) // GROUP

        @pl.loop(0, groups)
        def _(g):
            slots = [first + g * GROUP + n for n in range(GROUP)]
            for i in slots:
                tile_copy(i).wait()
            sums = [product(i) for i in slots]
            for i, value in zip(slots, sums):
                total[row[listed[i]] - first_row] += value

        @pl.loop(first + groups * GROUP, last)
        def _(i):
            tile_copy(i).wait()
            total[row[listed[i]] - first_row] += product(i)

        fetch(load + 1)

    if part:
        offset = 0
        for out in outs:
            length = out.shape[0]
            out[...] = total[offset : offset + length]
            offset += length


def slot_products(part, tables, tiles, panels, before=None):
    any_space = pl.BlockSpec(memory_space=pl.ANY)
    smem = pl.BlockSpec(memory_space=pltpu.SMEM)
    vmem = pl.BlockSpec(memory_space=pltpu.VMEM)
    block = lambda n: jax.ShapeDtypeStruct((n, EDGE, WIDTH), jnp.float32)
    scratch = [pltpu.VMEM((HELD, EDGE, EDGE), jnp.float32), pltpu.SemaphoreType.DMA((HELD,))]
    arrays = [tiles, panels]
    if part == 0:
        shapes = [block(BLOCKS)]
    else:
        shapes = [block(8)] if part == 1 else [block(8)] * 3
        rows = BLOCKS - FAR_ROW if part == 1 else FAR_ROW
        scratch = [pltpu.VMEM((rows, EDGE, WIDTH), jnp.float32)] + scratch
        arrays.append(before)
    share = (4, 1, 3)[part]
    return pl.pallas_call(
        functools.partial(products_kernel, part),
        out_shape=shapes,
        in_specs=[smem] * 4 + [any_space] + [vmem] * (len(arrays) - 1),
        out_specs=[vmem] * len(shapes),
        scratch_shapes=scratch,
        compiler_params=pltpu.CompilerParams(vmem_limit_bytes=LIMIT * 1024 * 1024),
        cost_estimate=pl.CostEstimate(
            flops=share * SLOTS * EDGE * EDGE * WIDTH,
            bytes_accessed=share * 3 * 1024 * 1024,
            transcendentals=0,
        ),
        name="slot_products",
    )(*tables, *arrays)


BAND = 64


def factor_kernel(gram, rows, embedding, factor, work):
    work[:, :WIDTH] = gram[...]
    work[:, WIDTH:] = rows[...].T
    lane = lax.broadcasted_iota(jnp.int32, (8, EDGE), 1)
    sub = lax.broadcasted_iota(jnp.int32, (8, EDGE), 0)
    columns = (WIDTH + EDGE) // EDGE

    def along_lanes(value, at):
        return jnp.broadcast_to(value[:, at : at + 1], (8, EDGE))

    def along_rows(value, at):
        return jnp.broadcast_to(value[at : at + 1, :], (8, EDGE))

    for band in range(WIDTH // BAND):
        top = band * BAND
        lead = top // EDGE
        strips = BAND // 8
        held = [
            [work[top + 8 * s : top + 8 * s + 8, c * EDGE : (c + 1) * EDGE] for c in range(lead, columns)]
            for s in range(strips)
        ]
        for s0 in range(strips):
            at = (top + 8 * s0) % EDGE
            cols = {s: [along_lanes(held[s][0], at + q) for q in range(8)] for s in range(s0, strips)}
            block = {(t, r): along_rows(cols[s0][r], t) for t in range(8) for r in range(t + 1)}
            lower = {}
            inverse = []
            root = []
            for q in range(8):
                inverse.append(1.0 / block[q, q])
                root.append(lax.rsqrt(block[q, q]))
                for t in range(q + 1, 8):
                    lower[t, q] = block[t, q] * inverse[q]
                for t in range(q + 1, 8):
                    for r in range(q + 1, t + 1):
                        block[t, r] = block[t, r] - lower[t, q] * block[r, q]
            lines = []
            for q in range(8):
                line = [along_rows(v, q) for v in held[s0]]
                for t in range(q):
                    line = [v - lower[q, t] * w for v, w in zip(line, lines[t])]
                lines.append(line)
            for s in range(s0 + 1, strips):
                weights = []
                for q in range(8):
                    value = cols[s][q]
                    for t in range(q):
                        value = value - lower[q, t] * weights[t]
                    weights.append(value)
                weights = [v * w for v, w in zip(weights, inverse)]
                for q in range(8):
                    held[s] = [v - weights[q] * w for v, w in zip(held[s], lines[q])]
            final = [jnp.zeros((8, EDGE), jnp.float32)] * len(held[s0])
            for q in range(8):
                final = [jnp.where(sub == q, w * root[q], v) for v, w in zip(final, lines[q])]
            for c in range(lead, columns):
                value = final[c - lead]
                if c < WIDTH // EDGE:
                    value = jnp.where(lane + c * EDGE >= sub + (top + 8 * s0), value, 0.0)
                work[top + 8 * s0 : top + 8 * s0 + 8, c * EDGE : (c + 1) * EDGE] = value
        below = top + BAND
        if below < WIDTH:
            base = below // EDGE * EDGE
            left = work[top:below, base:WIDTH]
            right = work[top:below, base:]
            update = lax.dot_general(
                left,
                right,
                (((0,), (0,)), ((), ())),
                precision=lax.Precision.HIGHEST,
                preferred_element_type=jnp.float32,
            )
            work[below:, base:] -= update[below - base :, :]
    scale = jnp.sqrt(jnp.float32(ROWS))
    for band in range(WIDTH // BAND):
        top = band * BAND
        lead = top // EDGE * EDGE
        if lead:
            factor[top : top + BAND, :lead] = jnp.zeros((BAND, lead), jnp.float32)
        factor[top : top + BAND, lead:] = work[top : top + BAND, lead:WIDTH] / scale
    embedding[...] = work[:, WIDTH:].T * scale


def factor_and_solve(gram, rows):
    vmem = pl.BlockSpec(memory_space=pltpu.VMEM)
    return pl.pallas_call(
        factor_kernel,
        out_shape=[
            jax.ShapeDtypeStruct((EDGE, WIDTH), jnp.float32),
            jax.ShapeDtypeStruct((WIDTH, WIDTH), jnp.float32),
        ],
        in_specs=[vmem, vmem],
        out_specs=[vmem, vmem],
        scratch_shapes=[pltpu.VMEM((WIDTH, WIDTH + EDGE), jnp.float32)],
        compiler_params=pltpu.CompilerParams(vmem_limit_bytes=16 * 1024 * 1024),
        name="factor_and_solve",
    )(gram, rows)


def exchange(value, axes):
    return lax.all_to_all(value, axes, 0, 0, tiled=True)


def on_device(tiles, tile_rows, tile_cols, bucket_fill, row_slot, sketch):
    here_x = lax.axis_index("x")
    here_z = lax.axis_index("z")
    here_core = lax.axis_index("core")

    slot_ids = jnp.arange(SLOTS, dtype=jnp.int32)
    bucket = slot_ids // PER_BUCKET
    cols = tile_cols[0, 0]
    side = (cols // 2 + here_core) % 2
    facing = 1 - 2 * (cols // 2)
    here_facing = 1 - 2 * here_core
    far_x = ((bucket // 8 - here_x) * facing) % 4
    far_z = ((bucket % 8 - here_z) * facing) % 8
    blk = jnp.where(cols % 2 == 0, far_z * 4 + far_x, 32 + far_x * 8 + far_z)
    block_ids = jnp.arange(BLOCKS, dtype=jnp.int32)
    target = jnp.sum(
        jnp.where(tile_rows[0, 0][:, None] == block_ids[None, :], row_slot[0][None, :], 0), axis=1
    )
    ahead = ((target // 8 - here_x) * here_facing) % 4
    chunk = jnp.where(ahead == 3, 1, jnp.where(ahead == 0, 0, ahead + 1))
    row = chunk * 8 + target % 8
    kind = jnp.where(side == 0, 0, jnp.where(row >= FAR_ROW, 1, 2))

    with jax.named_scope("gather"):
        mine = lax.dynamic_slice_in_dim(sketch, here_core * 2 * EDGE, 2 * EDGE, 0)
        slab = join(ring_gather(mine[:EDGE], "x"))
        line = join(ring_gather(mine[EDGE:], "z"))
        first = ring_gather(slab, "z")
        second = ring_gather(line, "x")
        slab, *plan, counts = lax.optimization_barrier((slab, *slot_plan(bucket_fill[0, 0], kind)))
        first[0] = slab
        early, final = [], []
        base = 0
        for found in (first, second):
            for distance, piece in enumerate(found):
                (final if distance == len(found) // 2 else early).append((base, piece))
                base += piece.shape[0]
        panels = place(final, base, place(early, base))
        panels_other = swap(panels)

    stack = tiles[0, 0]
    tables = [(counts, listed, blk, row) for listed in plan]
    (sums,) = slot_products(0, tables[0], stack, panels)
    (far,) = slot_products(1, tables[1], stack, panels_other, sums)
    own, behind, ahead = slot_products(2, tables[2], stack, panels_other, sums)

    with jax.named_scope("scatter_rows"):
        passing = shift(far, "x", 1)
        from_ahead = shift(behind, "x", -1)
        own = own + from_ahead + shift(ahead + passing, "x", 1)
        product_rows = jnp.sum(exchange(own, "z"), axis=0)

    with jax.named_scope("gram"):
        gram = jnp.dot(
            product_rows.T,
            product_rows,
            precision=lax.Precision.HIGHEST,
            preferred_element_type=jnp.float32,
        )
        ring = ("y", "core", "x")
        part = jnp.sum(exchange(gram, ring).reshape(32, 8, WIDTH), axis=0)
        part = jnp.sum(
            exchange(jnp.broadcast_to(part[None], (8, 8, WIDTH)), "z"), axis=0
        )
        gram = exchange(jnp.broadcast_to(part[None], (32, 8, WIDTH)), ring).reshape(WIDTH, WIDTH)

    embedding, factor = factor_and_solve(gram, product_rows)
    return embedding, factor


def solution(mesh):
    fine = Mesh(mesh.devices.reshape(SIZES), AXES)
    grp, col = ("y", "core"), ("x", "z")
    placed = (
        P(grp, col, None, None, None),
        P(grp, col, None),
        P(grp, col, None),
        P(grp, col, None),
        P(grp, None),
        P(col, None),
    )
    return jax.shard_map(
        on_device,
        mesh=fine,
        in_specs=placed,
        out_specs=(P(AXES, None), P()),
        check_vma=False,
    )
```

```python
import functools

import jax
import jax.numpy as jnp
from jax import lax
from jax.experimental import pallas as pl
from jax.experimental.pallas import tpu as pltpu
from jax.sharding import Mesh
from jax.sharding import PartitionSpec as P

AXES = ("y", "core", "x", "z")
SIZES = (4, 2, 4, 8)
EDGE = 128
WIDTH = 256
BLOCKS = 32
BUCKETS = 32
PER_BUCKET = 6
SLOTS = 192
ROWS = 32768
GROUP = 8
HELD = 96
LIMIT = 30
FAR_ROW = 24


def shift(value, axis, step):
    count = lax.axis_size(axis)
    pairs = [
        (core * count + i, core * count + (i + step - 2 * core * step) % count)
        for core in range(2)
        for i in range(count)
    ]
    return lax.ppermute(value, ("core", axis), pairs)


def swap(value):
    return lax.ppermute(value, "core", [(0, 1), (1, 0)])


def ring_gather(block, axis):
    count = lax.axis_size(axis)
    found = [None] * count
    found[0] = behind = ahead = block
    for step in range(1, count // 2):
        behind = shift(behind, axis, 1)
        ahead = shift(ahead, axis, -1)
        found[count - step] = behind
        found[step] = ahead
    behind, ahead = lax.optimization_barrier((behind, ahead))
    found[count // 2 + 1], found[count // 2 - 1] = behind, ahead
    found[count // 2] = shift(behind, axis, 1)
    return found


def join_kernel(*refs):
    out = refs[-1]
    offset = 0
    for piece in refs[:-1]:
        length = piece.shape[0]
        out[pl.ds(offset, length), :] = piece[...]
        offset += length


def join(pieces):
    total = sum(piece.shape[0] for piece in pieces)
    vmem = pl.BlockSpec(memory_space=pltpu.VMEM)
    return pl.pallas_call(
        join_kernel,
        out_shape=jax.ShapeDtypeStruct((total, WIDTH), jnp.float32),
        in_specs=[vmem] * len(pieces),
        out_specs=vmem,
        compiler_params=pltpu.CompilerParams(vmem_limit_bytes=8 * 1024 * 1024),
        cost_estimate=pl.CostEstimate(flops=0, bytes_accessed=total * WIDTH * 8, transcendentals=0),
        name="join",
    )(*pieces)


def place_kernel(offsets, late, *refs):
    pieces, out, sem = refs[late:-2], refs[-2], refs[-1]
    copies = [
        pltpu.make_async_copy(piece, out.at[pl.ds(offset, piece.shape[0])], sem.at[n])
        for n, (piece, offset) in enumerate(zip(pieces, offsets))
    ]
    for copy in copies:
        copy.start()
    for copy in copies:
        copy.wait()


def place(pieces, total, before=None):
    late = before is not None
    vmem = pl.BlockSpec(memory_space=pltpu.VMEM)
    any_space = pl.BlockSpec(memory_space=pl.ANY)
    offsets, arrays = zip(*pieces)
    moved = sum(array.size for array in arrays) * 8
    return pl.pallas_call(
        functools.partial(place_kernel, offsets, int(late)),
        out_shape=jax.ShapeDtypeStruct((total, WIDTH), jnp.float32),
        in_specs=[any_space] * late + [vmem] * len(arrays),
        out_specs=any_space,
        input_output_aliases={0: 0} if late else {},
        scratch_shapes=[pltpu.SemaphoreType.DMA((len(arrays),))],
        compiler_params=pltpu.CompilerParams(vmem_limit_bytes=16 * 1024 * 1024),
        cost_estimate=pl.CostEstimate(flops=0, bytes_accessed=moved, transcendentals=0),
        name="place",
    )(*([before] if late else []), *arrays)


def plan_kernel(fill, kind, *refs):
    plan, counts = refs[:3], refs[3]

    def list_bucket(b, ends):
        def put(j, ends):
            slot = b * PER_BUCKET + j
            which = kind[slot]
            for k in range(3):
                plan[k][ends[k]] = slot
            return tuple(e + (which == k).astype(jnp.int32) for k, e in enumerate(ends))

        return lax.fori_loop(0, fill[b], put, ends)

    ends = lax.fori_loop(0, BUCKETS, list_bucket, (0, 0, 0))
    for k in range(3):
        counts[k] = ends[k]


def slot_plan(fill, kind):
    smem = pl.BlockSpec(memory_space=pltpu.SMEM)
    return pl.pallas_call(
        plan_kernel,
        out_shape=[jax.ShapeDtypeStruct((SLOTS,), jnp.int32)] * 3
        + [jax.ShapeDtypeStruct((3,), jnp.int32)],
        in_specs=[smem, smem],
        out_specs=[smem] * 4,
        compiler_params=pltpu.CompilerParams(vmem_limit_bytes=1024 * 1024),
        cost_estimate=pl.CostEstimate(flops=0, bytes_accessed=12 * 1024 * 1024, transcendentals=0),
        name="slot_plan",
    )(fill, kind)


def products_kernel(part, counts, listed, blk, row, tiles, panels, *refs):
    first_row = FAR_ROW if part == 1 else 0
    if part == 0:
        total, held, tile_sem = refs
    else:
        before, outs = refs[0], refs[1:-3]
        total, held, tile_sem = refs[-3:]
    count = counts[part]

    def tile_copy(i):
        spot = lax.rem(i, HELD)
        return pltpu.make_async_copy(tiles.at[listed[i]], held.at[spot], tile_sem.at[spot])

    def fetch(load):
        @pl.loop(load * HELD, jnp.minimum((load + 1) * HELD, count))
        def _(i):
            tile_copy(i).start()

    fetch(0)
    total[...] = before[first_row : first_row + total.shape[0]] if part else jnp.zeros_like(total)

    def product(i):
        slot = listed[i]
        tile = held[lax.rem(i, HELD)]
        panel = panels[pl.ds(pl.multiple_of(blk[slot] * EDGE, EDGE), EDGE), :]
        tile_hi = tile.astype(jnp.bfloat16)
        tile_lo = (tile - tile_hi.astype(jnp.float32)).astype(jnp.bfloat16)
        panel_hi = panel.astype(jnp.bfloat16)
        panel_lo = (panel - panel_hi.astype(jnp.float32)).astype(jnp.bfloat16)
        left = jnp.concatenate([tile_hi, tile_hi, tile_lo], axis=1)
        right = jnp.concatenate([panel_hi, panel_lo, panel_hi], axis=0)
        return jnp.dot(left, right, preferred_element_type=jnp.float32)

    @pl.loop(0, pl.cdiv(count, HELD))
    def _(load):
        first = load * HELD
        last = jnp.minimum(first + HELD, count)
        groups = (last - first) // GROUP

        @pl.loop(0, groups)
        def _(g):
            slots = [first + g * GROUP + n for n in range(GROUP)]
            for i in slots:
                tile_copy(i).wait()
            sums = [product(i) for i in slots]
            for i, value in zip(slots, sums):
                total[row[listed[i]] - first_row] += value

        @pl.loop(first + groups * GROUP, last)
        def _(i):
            tile_copy(i).wait()
            total[row[listed[i]] - first_row] += product(i)

        fetch(load + 1)

    if part:
        offset = 0
        for out in outs:
            length = out.shape[0]
            out[...] = total[offset : offset + length]
            offset += length


def slot_products(part, tables, tiles, panels, before=None):
    any_space = pl.BlockSpec(memory_space=pl.ANY)
    smem = pl.BlockSpec(memory_space=pltpu.SMEM)
    vmem = pl.BlockSpec(memory_space=pltpu.VMEM)
    block = lambda n: jax.ShapeDtypeStruct((n, EDGE, WIDTH), jnp.float32)
    scratch = [pltpu.VMEM((HELD, EDGE, EDGE), jnp.float32), pltpu.SemaphoreType.DMA((HELD,))]
    arrays = [tiles, panels]
    if part == 0:
        shapes = [block(BLOCKS)]
    else:
        shapes = [block(8)] if part == 1 else [block(8)] * 3
        rows = BLOCKS - FAR_ROW if part == 1 else FAR_ROW
        scratch = [pltpu.VMEM((rows, EDGE, WIDTH), jnp.float32)] + scratch
        arrays.append(before)
    share = (4, 1, 3)[part]
    return pl.pallas_call(
        functools.partial(products_kernel, part),
        out_shape=shapes,
        in_specs=[smem] * 4 + [any_space] + [vmem] * (len(arrays) - 1),
        out_specs=[vmem] * len(shapes),
        scratch_shapes=scratch,
        compiler_params=pltpu.CompilerParams(vmem_limit_bytes=LIMIT * 1024 * 1024),
        cost_estimate=pl.CostEstimate(
            flops=share * SLOTS * EDGE * EDGE * WIDTH,
            bytes_accessed=share * 3 * 1024 * 1024,
            transcendentals=0,
        ),
        name="slot_products",
    )(*tables, *arrays)


BAND = 64


def factor_kernel(gram, rows, embedding, factor, work):
    work[:, :WIDTH] = gram[...]
    work[:, WIDTH:] = rows[...].T
    lane = lax.broadcasted_iota(jnp.int32, (8, EDGE), 1)
    sub = lax.broadcasted_iota(jnp.int32, (8, EDGE), 0)
    columns = (WIDTH + EDGE) // EDGE

    def along_lanes(value, at):
        return jnp.broadcast_to(value[:, at : at + 1], (8, EDGE))

    def along_rows(value, at):
        return jnp.broadcast_to(value[at : at + 1, :], (8, EDGE))

    for band in range(WIDTH // BAND):
        top = band * BAND
        lead = top // EDGE
        strips = BAND // 8
        held = [
            [work[top + 8 * s : top + 8 * s + 8, c * EDGE : (c + 1) * EDGE] for c in range(lead, columns)]
            for s in range(strips)
        ]
        for s0 in range(strips):
            at = (top + 8 * s0) % EDGE
            cols = {s: [along_lanes(held[s][0], at + q) for q in range(8)] for s in range(s0, strips)}
            block = {(t, r): along_rows(cols[s0][r], t) for t in range(8) for r in range(t + 1)}
            lower = {}
            inverse = []
            root = []
            for q in range(8):
                inverse.append(1.0 / block[q, q])
                root.append(lax.rsqrt(block[q, q]))
                for t in range(q + 1, 8):
                    lower[t, q] = block[t, q] * inverse[q]
                for t in range(q + 1, 8):
                    for r in range(q + 1, t + 1):
                        block[t, r] = block[t, r] - lower[t, q] * block[r, q]
            lines = []
            for q in range(8):
                line = [along_rows(v, q) for v in held[s0]]
                for t in range(q):
                    line = [v - lower[q, t] * w for v, w in zip(line, lines[t])]
                lines.append(line)
            for s in range(s0 + 1, strips):
                weights = []
                for q in range(8):
                    value = cols[s][q]
                    for t in range(q):
                        value = value - lower[q, t] * weights[t]
                    weights.append(value)
                weights = [v * w for v, w in zip(weights, inverse)]
                for c in range(len(held[s])):
                    terms = [weights[q] * lines[q][c] for q in range(8)]
                    while len(terms) > 1:
                        terms = [a + b for a, b in zip(terms[::2], terms[1::2])]
                    held[s][c] = held[s][c] - terms[0]
            final = [jnp.zeros((8, EDGE), jnp.float32)] * len(held[s0])
            for q in range(8):
                final = [jnp.where(sub == q, w * root[q], v) for v, w in zip(final, lines[q])]
            for c in range(lead, columns):
                value = final[c - lead]
                if c < WIDTH // EDGE:
                    value = jnp.where(lane + c * EDGE >= sub + (top + 8 * s0), value, 0.0)
                work[top + 8 * s0 : top + 8 * s0 + 8, c * EDGE : (c + 1) * EDGE] = value
        below = top + BAND
        if below < WIDTH:
            base = below // EDGE * EDGE
            left = work[top:below, base:WIDTH]
            right = work[top:below, base:]
            update = lax.dot_general(
                left,
                right,
                (((0,), (0,)), ((), ())),
                precision=lax.Precision.HIGHEST,
                preferred_element_type=jnp.float32,
            )
            work[below:, base:] -= update[below - base :, :]
    scale = jnp.sqrt(jnp.float32(ROWS))
    for band in range(WIDTH // BAND):
        top = band * BAND
        lead = top // EDGE * EDGE
        if lead:
            factor[top : top + BAND, :lead] = jnp.zeros((BAND, lead), jnp.float32)
        factor[top : top + BAND, lead:] = work[top : top + BAND, lead:WIDTH] / scale
    embedding[...] = work[:, WIDTH:].T * scale


def factor_and_solve(gram, rows):
    vmem = pl.BlockSpec(memory_space=pltpu.VMEM)
    return pl.pallas_call(
        factor_kernel,
        out_shape=[
            jax.ShapeDtypeStruct((EDGE, WIDTH), jnp.float32),
            jax.ShapeDtypeStruct((WIDTH, WIDTH), jnp.float32),
        ],
        in_specs=[vmem, vmem],
        out_specs=[vmem, vmem],
        scratch_shapes=[pltpu.VMEM((WIDTH, WIDTH + EDGE), jnp.float32)],
        compiler_params=pltpu.CompilerParams(vmem_limit_bytes=16 * 1024 * 1024),
        name="factor_and_solve",
    )(gram, rows)


def exchange(value, axes):
    return lax.all_to_all(value, axes, 0, 0, tiled=True)


def on_device(tiles, tile_rows, tile_cols, bucket_fill, row_slot, sketch):
    here_x = lax.axis_index("x")
    here_z = lax.axis_index("z")
    here_core = lax.axis_index("core")

    slot_ids = jnp.arange(SLOTS, dtype=jnp.int32)
    bucket = slot_ids // PER_BUCKET
    cols = tile_cols[0, 0]
    side = (cols // 2 + here_core) % 2
    facing = 1 - 2 * (cols // 2)
    here_facing = 1 - 2 * here_core
    far_x = ((bucket // 8 - here_x) * facing) % 4
    far_z = ((bucket % 8 - here_z) * facing) % 8
    blk = jnp.where(cols % 2 == 0, far_z * 4 + far_x, 32 + far_x * 8 + far_z)
    block_ids = jnp.arange(BLOCKS, dtype=jnp.int32)
    target = jnp.sum(
        jnp.where(tile_rows[0, 0][:, None] == block_ids[None, :], row_slot[0][None, :], 0), axis=1
    )
    ahead = ((target // 8 - here_x) * here_facing) % 4
    chunk = jnp.where(ahead == 3, 1, jnp.where(ahead == 0, 0, ahead + 1))
    row = chunk * 8 + ((target % 8 - here_z) * here_facing) % 8
    kind = jnp.where(side == 0, 0, jnp.where(row >= FAR_ROW, 1, 2))

    with jax.named_scope("gather"):
        mine = lax.dynamic_slice_in_dim(sketch, here_core * 2 * EDGE, 2 * EDGE, 0)
        top, low = mine[:EDGE], mine[EDGE:]
        top_behind, top_ahead, low_behind, low_ahead = lax.optimization_barrier(
            (shift(top, "x", 1), shift(top, "x", -1), shift(low, "z", 1), shift(low, "z", -1))
        )
        top_far, pair_behind, pair_ahead = lax.optimization_barrier(
            (
                shift(top_behind, "x", 1),
                shift(join([low_behind, low]), "z", 2),
                shift(join([low, low_ahead]), "z", -2),
            )
        )
        slab = join([top, top_ahead, top_far, top_behind])
        low_far = shift(pair_behind[:EDGE], "z", 1)
        line = join([low, low_ahead, pair_ahead, low_far, pair_behind, low_behind])
        first = ring_gather(slab, "z")
        second = ring_gather(line, "x")
        slab, *plan, counts = lax.optimization_barrier((slab, *slot_plan(bucket_fill[0, 0], kind)))
        first[0] = slab
        early, final = [], []
        base = 0
        for found in (first, second):
            for distance, piece in enumerate(found):
                (final if distance == len(found) // 2 else early).append((base, piece))
                base += piece.shape[0]
        panels = place(final, base, place(early, base))
        panels_other = swap(panels)

    stack = tiles[0, 0]
    tables = [(counts, listed, blk, row) for listed in plan]
    (sums,) = slot_products(0, tables[0], stack, panels)
    (far,) = slot_products(1, tables[1], stack, panels_other, sums)
    own, behind, ahead = slot_products(2, tables[2], stack, panels_other, sums)

    with jax.named_scope("scatter_rows"):
        passing = shift(far, "x", 1)
        from_ahead = shift(behind, "x", -1)
        own = own + from_ahead + shift(ahead + passing, "x", 1)
        passing = shift(own[4], "z", 1)
        ahead = jnp.stack([own[2], own[3] + passing])
        ahead, behind = lax.optimization_barrier((ahead, own[5:7]))
        ahead, behind = shift(ahead, "z", 2), shift(behind, "z", -2)
        middle = own[0] + ahead[0] + behind[1]
        ahead, behind = lax.optimization_barrier((own[1] + ahead[1], own[7] + behind[0]))
        product_rows = middle + shift(ahead, "z", 1) + shift(behind, "z", -1)

    with jax.named_scope("gram"):
        gram = jnp.dot(
            product_rows.T,
            product_rows,
            precision=lax.Precision.HIGHEST,
            preferred_element_type=jnp.float32,
        )
        ring = ("y", "core", "x")
        part = jnp.sum(exchange(gram, ring).reshape(32, 8, WIDTH), axis=0)
        part = jnp.sum(
            exchange(jnp.broadcast_to(part[None], (8, 8, WIDTH)), "z"), axis=0
        )
        gram = exchange(jnp.broadcast_to(part[None], (32, 8, WIDTH)), ring).reshape(WIDTH, WIDTH)

    embedding, factor = factor_and_solve(gram, product_rows)
    return embedding, factor


def solution(mesh):
    fine = Mesh(mesh.devices.reshape(SIZES), AXES)
    grp, col = ("y", "core"), ("x", "z")
    placed = (
        P(grp, col, None, None, None),
        P(grp, col, None),
        P(grp, col, None),
        P(grp, col, None),
        P(grp, None),
        P(col, None),
    )
    return jax.shard_map(
        on_device,
        mesh=fine,
        in_specs=placed,
        out_specs=(P(AXES, None), P()),
        check_vma=False,
    )
```

```python
import functools

import jax
import jax.numpy as jnp
from jax import lax
from jax.experimental import pallas as pl
from jax.experimental.pallas import tpu as pltpu
from jax.sharding import Mesh
from jax.sharding import PartitionSpec as P

AXES = ("y", "core", "x", "z")
SIZES = (4, 2, 4, 8)
EDGE = 128
WIDTH = 256
BLOCKS = 32
BUCKETS = 32
PER_BUCKET = 6
SLOTS = 192
ROWS = 32768
GROUP = 8
HELD = 96
LIMIT = 30
FAR_ROW = 24


def shift(value, axis, step):
    count = lax.axis_size(axis)
    pairs = [
        (core * count + i, core * count + (i + step - 2 * core * step) % count)
        for core in range(2)
        for i in range(count)
    ]
    return lax.ppermute(value, ("core", axis), pairs)


def swap(value):
    return lax.ppermute(value, "core", [(0, 1), (1, 0)])


def join_rows(top, bottom):
    return jnp.concatenate([top, bottom], axis=0)


def ring_gather(block, axis):
    count = lax.axis_size(axis)
    found = [None] * count
    found[0] = behind = ahead = block
    for step in range(1, count // 2):
        behind = shift(behind, axis, 1)
        ahead = shift(ahead, axis, -1)
        found[count - step] = behind
        found[step] = ahead
    behind, ahead = lax.optimization_barrier((behind, ahead))
    found[count // 2 + 1], found[count // 2 - 1] = behind, ahead
    found[count // 2] = shift(behind, axis, 1)
    return found


def join_kernel(*refs):
    out = refs[-1]
    offset = 0
    for piece in refs[:-1]:
        length = piece.shape[0]
        out[pl.ds(offset, length), :] = piece[...]
        offset += length


def join(pieces):
    total = sum(piece.shape[0] for piece in pieces)
    vmem = pl.BlockSpec(memory_space=pltpu.VMEM)
    return pl.pallas_call(
        join_kernel,
        out_shape=jax.ShapeDtypeStruct((total, WIDTH), jnp.float32),
        in_specs=[vmem] * len(pieces),
        out_specs=vmem,
        compiler_params=pltpu.CompilerParams(vmem_limit_bytes=8 * 1024 * 1024),
        cost_estimate=pl.CostEstimate(flops=0, bytes_accessed=total * WIDTH * 8, transcendentals=0),
        name="join",
    )(*pieces)


def place_kernel(offsets, late, *refs):
    pieces, out, sem = refs[late:-2], refs[-2], refs[-1]
    copies = [
        pltpu.make_async_copy(piece, out.at[pl.ds(offset, piece.shape[0])], sem.at[n])
        for n, (piece, offset) in enumerate(zip(pieces, offsets))
    ]
    for copy in copies:
        copy.start()
    for copy in copies:
        copy.wait()


def place(pieces, total, before=None):
    late = before is not None
    vmem = pl.BlockSpec(memory_space=pltpu.VMEM)
    any_space = pl.BlockSpec(memory_space=pl.ANY)
    offsets, arrays = zip(*pieces)
    moved = sum(array.size for array in arrays) * 8
    return pl.pallas_call(
        functools.partial(place_kernel, offsets, int(late)),
        out_shape=jax.ShapeDtypeStruct((total, WIDTH), jnp.float32),
        in_specs=[any_space] * late + [vmem] * len(arrays),
        out_specs=any_space,
        input_output_aliases={0: 0} if late else {},
        scratch_shapes=[pltpu.SemaphoreType.DMA((len(arrays),))],
        compiler_params=pltpu.CompilerParams(vmem_limit_bytes=16 * 1024 * 1024),
        cost_estimate=pl.CostEstimate(flops=0, bytes_accessed=moved, transcendentals=0),
        name="place",
    )(*([before] if late else []), *arrays)


def plan_kernel(fill, kind, *refs):
    plan, counts = refs[:3], refs[3]

    def list_bucket(b, ends):
        def put(j, ends):
            slot = b * PER_BUCKET + j
            which = kind[slot]
            for k in range(3):
                plan[k][ends[k]] = slot
            return tuple(e + (which == k).astype(jnp.int32) for k, e in enumerate(ends))

        return lax.fori_loop(0, fill[b], put, ends)

    ends = lax.fori_loop(0, BUCKETS, list_bucket, (0, 0, 0))
    for k in range(3):
        counts[k] = ends[k]


def slot_plan(fill, kind):
    smem = pl.BlockSpec(memory_space=pltpu.SMEM)
    return pl.pallas_call(
        plan_kernel,
        out_shape=[jax.ShapeDtypeStruct((SLOTS,), jnp.int32)] * 3
        + [jax.ShapeDtypeStruct((3,), jnp.int32)],
        in_specs=[smem, smem],
        out_specs=[smem] * 4,
        compiler_params=pltpu.CompilerParams(vmem_limit_bytes=1024 * 1024),
        cost_estimate=pl.CostEstimate(flops=0, bytes_accessed=12 * 1024 * 1024, transcendentals=0),
        name="slot_plan",
    )(fill, kind)


def products_kernel(part, counts, listed, blk, row, tiles, panels, *refs):
    first_row = FAR_ROW if part == 1 else 0
    if part == 0:
        total, held, tile_sem = refs
    else:
        before, outs = refs[0], refs[1:-3]
        total, held, tile_sem = refs[-3:]
    count = counts[part]

    def tile_copy(i):
        spot = lax.rem(i, HELD)
        return pltpu.make_async_copy(tiles.at[listed[i]], held.at[spot], tile_sem.at[spot])

    def fetch(load):
        @pl.loop(load * HELD, jnp.minimum((load + 1) * HELD, count))
        def _(i):
            tile_copy(i).start()

    fetch(0)
    total[...] = before[first_row : first_row + total.shape[0]] if part else jnp.zeros_like(total)

    def product(i):
        slot = listed[i]
        tile = held[lax.rem(i, HELD)]
        panel = panels[pl.ds(pl.multiple_of(blk[slot] * EDGE, EDGE), EDGE), :]
        tile_hi = tile.astype(jnp.bfloat16)
        tile_lo = (tile - tile_hi.astype(jnp.float32)).astype(jnp.bfloat16)
        panel_hi = panel.astype(jnp.bfloat16)
        panel_lo = (panel - panel_hi.astype(jnp.float32)).astype(jnp.bfloat16)
        left = jnp.concatenate([tile_hi, tile_hi, tile_lo], axis=1)
        right = jnp.concatenate([panel_hi, panel_lo, panel_hi], axis=0)
        return jnp.dot(left, right, preferred_element_type=jnp.float32)

    @pl.loop(0, pl.cdiv(count, HELD))
    def _(load):
        first = load * HELD
        last = jnp.minimum(first + HELD, count)
        groups = (last - first) // GROUP

        @pl.loop(0, groups)
        def _(g):
            slots = [first + g * GROUP + n for n in range(GROUP)]
            for i in slots:
                tile_copy(i).wait()
            sums = [product(i) for i in slots]
            for i, value in zip(slots, sums):
                total[row[listed[i]] - first_row] += value

        @pl.loop(first + groups * GROUP, last)
        def _(i):
            tile_copy(i).wait()
            total[row[listed[i]] - first_row] += product(i)

        fetch(load + 1)

    if part:
        offset = 0
        for out in outs:
            length = out.shape[0]
            out[...] = total[offset : offset + length]
            offset += length


def slot_products(part, tables, tiles, panels, before=None):
    any_space = pl.BlockSpec(memory_space=pl.ANY)
    smem = pl.BlockSpec(memory_space=pltpu.SMEM)
    vmem = pl.BlockSpec(memory_space=pltpu.VMEM)
    block = lambda n: jax.ShapeDtypeStruct((n, EDGE, WIDTH), jnp.float32)
    scratch = [pltpu.VMEM((HELD, EDGE, EDGE), jnp.float32), pltpu.SemaphoreType.DMA((HELD,))]
    arrays = [tiles, panels]
    if part == 0:
        shapes = [block(BLOCKS)]
    else:
        shapes = [block(8)] if part == 1 else [block(8)] * 3
        rows = BLOCKS - FAR_ROW if part == 1 else FAR_ROW
        scratch = [pltpu.VMEM((rows, EDGE, WIDTH), jnp.float32)] + scratch
        arrays.append(before)
    share = (4, 1, 3)[part]
    return pl.pallas_call(
        functools.partial(products_kernel, part),
        out_shape=shapes,
        in_specs=[smem] * 4 + [any_space] + [vmem] * (len(arrays) - 1),
        out_specs=[vmem] * len(shapes),
        scratch_shapes=scratch,
        compiler_params=pltpu.CompilerParams(vmem_limit_bytes=LIMIT * 1024 * 1024),
        cost_estimate=pl.CostEstimate(
            flops=share * SLOTS * EDGE * EDGE * WIDTH,
            bytes_accessed=share * 3 * 1024 * 1024,
            transcendentals=0,
        ),
        name="slot_products",
    )(*tables, *arrays)


BAND = 64


def factor_kernel(gram, rows, embedding, factor, work):
    work[:, :WIDTH] = gram[...]
    work[:, WIDTH:] = rows[...].T
    lane = lax.broadcasted_iota(jnp.int32, (8, EDGE), 1)
    sub = lax.broadcasted_iota(jnp.int32, (8, EDGE), 0)
    columns = (WIDTH + EDGE) // EDGE

    def along_lanes(value, at):
        return jnp.broadcast_to(value[:, at : at + 1], (8, EDGE))

    def along_rows(value, at):
        return jnp.broadcast_to(value[at : at + 1, :], (8, EDGE))

    for band in range(WIDTH // BAND):
        top = band * BAND
        lead = top // EDGE
        strips = BAND // 8
        held = [
            [work[top + 8 * s : top + 8 * s + 8, c * EDGE : (c + 1) * EDGE] for c in range(lead, columns)]
            for s in range(strips)
        ]
        for s0 in range(strips):
            at = (top + 8 * s0) % EDGE
            cols = {s: [along_lanes(held[s][0], at + q) for q in range(8)] for s in range(s0, strips)}
            block = {(t, r): along_rows(cols[s0][r], t) for t in range(8) for r in range(t + 1)}
            lower = {}
            inverse = []
            root = []
            for q in range(8):
                inverse.append(1.0 / block[q, q])
                root.append(lax.rsqrt(block[q, q]))
                for t in range(q + 1, 8):
                    lower[t, q] = block[t, q] * inverse[q]
                for t in range(q + 1, 8):
                    for r in range(q + 1, t + 1):
                        block[t, r] = block[t, r] - lower[t, q] * block[r, q]
            lines = []
            for q in range(8):
                line = [along_rows(v, q) for v in held[s0]]
                for t in range(q):
                    line = [v - lower[q, t] * w for v, w in zip(line, lines[t])]
                lines.append(line)
            for s in range(s0 + 1, strips):
                weights = []
                for q in range(8):
                    value = cols[s][q]
                    for t in range(q):
                        value = value - lower[q, t] * weights[t]
                    weights.append(value)
                weights = [v * w for v, w in zip(weights, inverse)]
                for c in range(len(held[s])):
                    terms = [weights[q] * lines[q][c] for q in range(8)]
                    while len(terms) > 1:
                        terms = [a + b for a, b in zip(terms[::2], terms[1::2])]
                    held[s][c] = held[s][c] - terms[0]
            final = [jnp.zeros((8, EDGE), jnp.float32)] * len(held[s0])
            for q in range(8):
                final = [jnp.where(sub == q, w * root[q], v) for v, w in zip(final, lines[q])]
            for c in range(lead, columns):
                value = final[c - lead]
                if c < WIDTH // EDGE:
                    value = jnp.where(lane + c * EDGE >= sub + (top + 8 * s0), value, 0.0)
                work[top + 8 * s0 : top + 8 * s0 + 8, c * EDGE : (c + 1) * EDGE] = value
        below = top + BAND
        if below < WIDTH:
            base = below // EDGE * EDGE
            left = work[top:below, base:WIDTH]
            right = work[top:below, base:]
            update = lax.dot_general(
                left,
                right,
                (((0,), (0,)), ((), ())),
                precision=lax.Precision.HIGHEST,
                preferred_element_type=jnp.float32,
            )
            work[below:, base:] -= update[below - base :, :]
    scale = jnp.sqrt(jnp.float32(ROWS))
    for band in range(WIDTH // BAND):
        top = band * BAND
        lead = top // EDGE * EDGE
        if lead:
            factor[top : top + BAND, :lead] = jnp.zeros((BAND, lead), jnp.float32)
        factor[top : top + BAND, lead:] = work[top : top + BAND, lead:WIDTH] / scale
    embedding[...] = work[:, WIDTH:].T * scale


def factor_and_solve(gram, rows):
    vmem = pl.BlockSpec(memory_space=pltpu.VMEM)
    return pl.pallas_call(
        factor_kernel,
        out_shape=[
            jax.ShapeDtypeStruct((EDGE, WIDTH), jnp.float32),
            jax.ShapeDtypeStruct((WIDTH, WIDTH), jnp.float32),
        ],
        in_specs=[vmem, vmem],
        out_specs=[vmem, vmem],
        scratch_shapes=[pltpu.VMEM((WIDTH, WIDTH + EDGE), jnp.float32)],
        compiler_params=pltpu.CompilerParams(vmem_limit_bytes=16 * 1024 * 1024),
        name="factor_and_solve",
    )(gram, rows)


def exchange(value, axes):
    return lax.all_to_all(value, axes, 0, 0, tiled=True)


def on_device(tiles, tile_rows, tile_cols, bucket_fill, row_slot, sketch):
    here_x = lax.axis_index("x")
    here_z = lax.axis_index("z")
    here_core = lax.axis_index("core")

    slot_ids = jnp.arange(SLOTS, dtype=jnp.int32)
    bucket = slot_ids // PER_BUCKET
    cols = tile_cols[0, 0]
    side = (cols // 2 + here_core) % 2
    facing = 1 - 2 * (cols // 2)
    here_facing = 1 - 2 * here_core
    far_x = ((bucket // 8 - here_x) * facing) % 4
    far_z = ((bucket % 8 - here_z) * facing) % 8
    blk = jnp.where(cols % 2 == 0, far_z * 4 + far_x, 32 + far_x * 8 + far_z)
    block_ids = jnp.arange(BLOCKS, dtype=jnp.int32)
    target = jnp.sum(
        jnp.where(tile_rows[0, 0][:, None] == block_ids[None, :], row_slot[0][None, :], 0), axis=1
    )
    ahead = ((target // 8 - here_x) * here_facing) % 4
    chunk = jnp.where(ahead == 3, 1, jnp.where(ahead == 0, 0, ahead + 1))
    row = chunk * 8 + ((target % 8 - here_z) * here_facing) % 8
    kind = jnp.where(side == 0, 0, jnp.where(row >= FAR_ROW, 1, 2))

    with jax.named_scope("gather"):
        mine = lax.dynamic_slice_in_dim(sketch, here_core * 2 * EDGE, 2 * EDGE, 0)
        slab = join(ring_gather(mine[:EDGE], "x"))
        line = join(ring_gather(mine[EDGE:], "z"))
        first = ring_gather(slab, "z")
        second = ring_gather(line, "x")
        slab, *plan, counts = lax.optimization_barrier((slab, *slot_plan(bucket_fill[0, 0], kind)))
        first[0] = slab
        early, final = [], []
        base = 0
        for found in (first, second):
            for distance, piece in enumerate(found):
                (final if distance == len(found) // 2 else early).append((base, piece))
                base += piece.shape[0]
        panels = place(final, base, place(early, base))
        panels_other = swap(panels)

    stack = tiles[0, 0]
    tables = [(counts, listed, blk, row) for listed in plan]
    (sums,) = slot_products(0, tables[0], stack, panels)
    (far,) = slot_products(1, tables[1], stack, panels_other, sums)
    own, behind, ahead = slot_products(2, tables[2], stack, panels_other, sums)

    with jax.named_scope("scatter_rows"):
        passing = shift(far, "x", 1)
        from_ahead = shift(behind, "x", -1)
        low, high = ahead[:4] + passing[:4], ahead[4:] + passing[4:]
        low, high = lax.optimization_barrier((low, high))
        own = own + from_ahead + join_rows(shift(low, "x", 1), shift(high, "x", 1))
        passing = shift(own[4], "z", 1)
        ahead = jnp.stack([own[2], own[3] + passing])
        ahead, behind = lax.optimization_barrier((ahead, own[5:7]))
        ahead, behind = shift(ahead, "z", 2), shift(behind, "z", -2)
        middle = own[0] + ahead[0] + behind[1]
        ahead, behind = lax.optimization_barrier((own[1] + ahead[1], own[7] + behind[0]))
        product_rows = middle + shift(ahead, "z", 1) + shift(behind, "z", -1)

    with jax.named_scope("gram"):
        gram = jnp.dot(
            product_rows.T,
            product_rows,
            precision=lax.Precision.HIGHEST,
            preferred_element_type=jnp.float32,
        )
        ring = ("y", "core", "x")
        part = jnp.sum(exchange(gram, ring).reshape(32, 8, WIDTH), axis=0)
        part = jnp.sum(
            exchange(jnp.broadcast_to(part[None], (8, 8, WIDTH)), "z"), axis=0
        )
        gram = exchange(jnp.broadcast_to(part[None], (32, 8, WIDTH)), ring).reshape(WIDTH, WIDTH)

    embedding, factor = factor_and_solve(gram, product_rows)
    return embedding, factor


def solution(mesh):
    fine = Mesh(mesh.devices.reshape(SIZES), AXES)
    grp, col = ("y", "core"), ("x", "z")
    placed = (
        P(grp, col, None, None, None),
        P(grp, col, None),
        P(grp, col, None),
        P(grp, col, None),
        P(grp, None),
        P(col, None),
    )
    return jax.shard_map(
        on_device,
        mesh=fine,
        in_specs=placed,
        out_specs=(P(AXES, None), P()),
        check_vma=False,
    )
```

```python
import functools

import jax
import jax.numpy as jnp
from jax import lax
from jax.experimental import pallas as pl
from jax.experimental.pallas import tpu as pltpu
from jax.sharding import Mesh
from jax.sharding import PartitionSpec as P

AXES = ("y", "core", "x", "z")
SIZES = (4, 2, 4, 8)
EDGE = 128
WIDTH = 256
BLOCKS = 32
BUCKETS = 32
PER_BUCKET = 6
SLOTS = 192
ROWS = 32768
GROUP = 8
HELD = 96
LIMIT = 30
PARTS = 2


def shift(value, axis, step):
    count = lax.axis_size(axis)
    pairs = [
        (core * count + i, core * count + (i + step - 2 * core * step) % count)
        for core in range(2)
        for i in range(count)
    ]
    return lax.ppermute(value, ("core", axis), pairs)


def swap(value):
    return lax.ppermute(value, "core", [(0, 1), (1, 0)])


def ring_gather(block, axis):
    count = lax.axis_size(axis)
    found = [None] * count
    found[0] = behind = ahead = block
    for step in range(1, count // 2):
        behind = shift(behind, axis, 1)
        ahead = shift(ahead, axis, -1)
        found[count - step] = behind
        found[step] = ahead
    behind, ahead = lax.optimization_barrier((behind, ahead))
    found[count // 2 + 1], found[count // 2 - 1] = behind, ahead
    found[count // 2] = shift(behind, axis, 1)
    return found


def join_kernel(*refs):
    out = refs[-1]
    offset = 0
    for piece in refs[:-1]:
        length = piece.shape[0]
        out[pl.ds(offset, length), :] = piece[...]
        offset += length


def join(pieces):
    total = sum(piece.shape[0] for piece in pieces)
    vmem = pl.BlockSpec(memory_space=pltpu.VMEM)
    return pl.pallas_call(
        join_kernel,
        out_shape=jax.ShapeDtypeStruct((total, WIDTH), jnp.float32),
        in_specs=[vmem] * len(pieces),
        out_specs=vmem,
        compiler_params=pltpu.CompilerParams(vmem_limit_bytes=8 * 1024 * 1024),
        cost_estimate=pl.CostEstimate(flops=0, bytes_accessed=total * WIDTH * 8, transcendentals=0),
        name="join",
    )(*pieces)


def place_kernel(offsets, late, *refs):
    pieces, out, sem = refs[late:-2], refs[-2], refs[-1]
    copies = [
        pltpu.make_async_copy(piece, out.at[pl.ds(offset, piece.shape[0])], sem.at[n])
        for n, (piece, offset) in enumerate(zip(pieces, offsets))
    ]
    for copy in copies:
        copy.start()
    for copy in copies:
        copy.wait()


def place(pieces, total, before=None):
    late = before is not None
    vmem = pl.BlockSpec(memory_space=pltpu.VMEM)
    any_space = pl.BlockSpec(memory_space=pl.ANY)
    offsets, arrays = zip(*pieces)
    moved = sum(array.size for array in arrays) * 8
    return pl.pallas_call(
        functools.partial(place_kernel, offsets, int(late)),
        out_shape=jax.ShapeDtypeStruct((total, WIDTH), jnp.float32),
        in_specs=[any_space] * late + [vmem] * len(arrays),
        out_specs=any_space,
        input_output_aliases={0: 0} if late else {},
        scratch_shapes=[pltpu.SemaphoreType.DMA((len(arrays),))],
        compiler_params=pltpu.CompilerParams(vmem_limit_bytes=16 * 1024 * 1024),
        cost_estimate=pl.CostEstimate(flops=0, bytes_accessed=moved, transcendentals=0),
        name="place",
    )(*([before] if late else []), *arrays)


def plan_kernel(fill, side, *refs):
    plan, counts = refs[:PARTS], refs[PARTS]

    def list_bucket(b, ends):
        def put(j, ends):
            slot = b * PER_BUCKET + j
            which = side[slot]
            for k in range(PARTS):
                plan[k][ends[k]] = slot
            return tuple(e + (which == k).astype(jnp.int32) for k, e in enumerate(ends))

        return lax.fori_loop(0, fill[b], put, ends)

    ends = lax.fori_loop(0, BUCKETS, list_bucket, (0,) * PARTS)
    for k in range(PARTS):
        counts[k] = ends[k]


def slot_plan(fill, side):
    smem = pl.BlockSpec(memory_space=pltpu.SMEM)
    return pl.pallas_call(
        plan_kernel,
        out_shape=[jax.ShapeDtypeStruct((SLOTS,), jnp.int32)] * PARTS
        + [jax.ShapeDtypeStruct((PARTS,), jnp.int32)],
        in_specs=[smem, smem],
        out_specs=[smem] * (PARTS + 1),
        compiler_params=pltpu.CompilerParams(vmem_limit_bytes=1024 * 1024),
        cost_estimate=pl.CostEstimate(flops=0, bytes_accessed=12 * 1024 * 1024, transcendentals=0),
        name="slot_plan",
    )(fill, side)


def products_kernel(part, counts, listed, blk, row, tiles, panels, *refs):
    if part == 0:
        total, held, tile_sem = refs
    else:
        before, outs = refs[0], refs[1:-3]
        total, held, tile_sem = refs[-3:]
    count = counts[part]

    def tile_copy(i):
        spot = lax.rem(i, HELD)
        return pltpu.make_async_copy(tiles.at[listed[i]], held.at[spot], tile_sem.at[spot])

    def fetch(load):
        @pl.loop(load * HELD, jnp.minimum((load + 1) * HELD, count))
        def _(i):
            tile_copy(i).start()

    fetch(0)
    total[...] = before[...] if part else jnp.zeros_like(total)

    def product(i):
        slot = listed[i]
        tile = held[lax.rem(i, HELD)]
        panel = panels[pl.ds(pl.multiple_of(blk[slot] * EDGE, EDGE), EDGE), :]
        tile_hi = tile.astype(jnp.bfloat16)
        tile_lo = (tile - tile_hi.astype(jnp.float32)).astype(jnp.bfloat16)
        panel_hi = panel.astype(jnp.bfloat16)
        panel_lo = (panel - panel_hi.astype(jnp.float32)).astype(jnp.bfloat16)
        left = jnp.concatenate([tile_hi, tile_hi, tile_lo], axis=1)
        right = jnp.concatenate([panel_hi, panel_lo, panel_hi], axis=0)
        return jnp.dot(left, right, preferred_element_type=jnp.float32)

    @pl.loop(0, pl.cdiv(count, HELD))
    def _(load):
        first = load * HELD
        last = jnp.minimum(first + HELD, count)
        groups = (last - first) // GROUP

        @pl.loop(0, groups)
        def _(g):
            slots = [first + g * GROUP + n for n in range(GROUP)]
            for i in slots:
                tile_copy(i).wait()
            sums = [product(i) for i in slots]
            for i, value in zip(slots, sums):
                total[row[listed[i]]] += value

        @pl.loop(first + groups * GROUP, last)
        def _(i):
            tile_copy(i).wait()
            total[row[listed[i]]] += product(i)

        fetch(load + 1)

    if part:
        offset = 0
        for out in outs:
            length = out.shape[0]
            out[...] = total[offset : offset + length]
            offset += length


def slot_products(part, tables, tiles, panels, before=None):
    any_space = pl.BlockSpec(memory_space=pl.ANY)
    smem = pl.BlockSpec(memory_space=pltpu.SMEM)
    vmem = pl.BlockSpec(memory_space=pltpu.VMEM)
    block = lambda n: jax.ShapeDtypeStruct((n, EDGE, WIDTH), jnp.float32)
    scratch = [pltpu.VMEM((HELD, EDGE, EDGE), jnp.float32), pltpu.SemaphoreType.DMA((HELD,))]
    arrays = [tiles, panels]
    if part == 0:
        shapes = [block(BLOCKS)]
    else:
        shapes = [block(8)] * 4
        scratch = [pltpu.VMEM((BLOCKS, EDGE, WIDTH), jnp.float32)] + scratch
        arrays.append(before)
    return pl.pallas_call(
        functools.partial(products_kernel, part),
        out_shape=shapes,
        in_specs=[smem] * 4 + [any_space] + [vmem] * (len(arrays) - 1),
        out_specs=[vmem] * len(shapes),
        scratch_shapes=scratch,
        compiler_params=pltpu.CompilerParams(vmem_limit_bytes=LIMIT * 1024 * 1024),
        cost_estimate=pl.CostEstimate(
            flops=4 * SLOTS * EDGE * EDGE * WIDTH,
            bytes_accessed=12 * 1024 * 1024,
            transcendentals=0,
        ),
        name="slot_products",
    )(*tables, *arrays)


BAND = 64


def factor_kernel(gram, rows, embedding, factor, work):
    work[:, :WIDTH] = gram[...]
    work[:, WIDTH:] = rows[...].T
    lane = lax.broadcasted_iota(jnp.int32, (8, EDGE), 1)
    sub = lax.broadcasted_iota(jnp.int32, (8, EDGE), 0)
    columns = (WIDTH + EDGE) // EDGE

    def along_lanes(value, at):
        return jnp.broadcast_to(value[:, at : at + 1], (8, EDGE))

    def along_rows(value, at):
        return jnp.broadcast_to(value[at : at + 1, :], (8, EDGE))

    for band in range(WIDTH // BAND):
        top = band * BAND
        lead = top // EDGE
        strips = BAND // 8
        held = [
            [work[top + 8 * s : top + 8 * s + 8, c * EDGE : (c + 1) * EDGE] for c in range(lead, columns)]
            for s in range(strips)
        ]
        for s0 in range(strips):
            at = (top + 8 * s0) % EDGE
            cols = {s: [along_lanes(held[s][0], at + q) for q in range(8)] for s in range(s0, strips)}
            block = {(t, r): along_rows(cols[s0][r], t) for t in range(8) for r in range(t + 1)}
            lower = {}
            inverse = []
            root = []
            for q in range(8):
                inverse.append(1.0 / block[q, q])
                root.append(lax.rsqrt(block[q, q]))
                for t in range(q + 1, 8):
                    lower[t, q] = block[t, q] * inverse[q]
                for t in range(q + 1, 8):
                    for r in range(q + 1, t + 1):
                        block[t, r] = block[t, r] - lower[t, q] * block[r, q]
            lines = []
            for q in range(8):
                line = [along_rows(v, q) for v in held[s0]]
                for t in range(q):
                    line = [v - lower[q, t] * w for v, w in zip(line, lines[t])]
                lines.append(line)
            for s in range(s0 + 1, strips):
                weights = []
                for q in range(8):
                    value = cols[s][q]
                    for t in range(q):
                        value = value - lower[q, t] * weights[t]
                    weights.append(value)
                weights = [v * w for v, w in zip(weights, inverse)]
                for c in range(len(held[s])):
                    terms = [weights[q] * lines[q][c] for q in range(8)]
                    while len(terms) > 1:
                        terms = [a + b for a, b in zip(terms[::2], terms[1::2])]
                    held[s][c] = held[s][c] - terms[0]
            final = [jnp.zeros((8, EDGE), jnp.float32)] * len(held[s0])
            for q in range(8):
                final = [jnp.where(sub == q, w * root[q], v) for v, w in zip(final, lines[q])]
            for c in range(lead, columns):
                value = final[c - lead]
                if c < WIDTH // EDGE:
                    value = jnp.where(lane + c * EDGE >= sub + (top + 8 * s0), value, 0.0)
                work[top + 8 * s0 : top + 8 * s0 + 8, c * EDGE : (c + 1) * EDGE] = value
        below = top + BAND
        if below < WIDTH:
            base = below // EDGE * EDGE
            left = work[top:below, base:WIDTH]
            right = work[top:below, base:]
            update = lax.dot_general(
                left,
                right,
                (((0,), (0,)), ((), ())),
                precision=lax.Precision.HIGHEST,
                preferred_element_type=jnp.float32,
            )
            work[below:, base:] -= update[below - base :, :]
    scale = jnp.sqrt(jnp.float32(ROWS))
    for band in range(WIDTH // BAND):
        top = band * BAND
        lead = top // EDGE * EDGE
        if lead:
            factor[top : top + BAND, :lead] = jnp.zeros((BAND, lead), jnp.float32)
        factor[top : top + BAND, lead:] = work[top : top + BAND, lead:WIDTH] / scale
    embedding[...] = work[:, WIDTH:].T * scale


def factor_and_solve(gram, rows):
    vmem = pl.BlockSpec(memory_space=pltpu.VMEM)
    return pl.pallas_call(
        factor_kernel,
        out_shape=[
            jax.ShapeDtypeStruct((EDGE, WIDTH), jnp.float32),
            jax.ShapeDtypeStruct((WIDTH, WIDTH), jnp.float32),
        ],
        in_specs=[vmem, vmem],
        out_specs=[vmem, vmem],
        scratch_shapes=[pltpu.VMEM((WIDTH, WIDTH + EDGE), jnp.float32)],
        compiler_params=pltpu.CompilerParams(vmem_limit_bytes=16 * 1024 * 1024),
        name="factor_and_solve",
    )(gram, rows)


def exchange(value, axes):
    return lax.all_to_all(value, axes, 0, 0, tiled=True)


def on_device(tiles, tile_rows, tile_cols, bucket_fill, row_slot, sketch):
    here_x = lax.axis_index("x")
    here_z = lax.axis_index("z")
    here_core = lax.axis_index("core")

    slot_ids = jnp.arange(SLOTS, dtype=jnp.int32)
    bucket = slot_ids // PER_BUCKET
    cols = tile_cols[0, 0]
    side = (cols // 2 + here_core) % 2
    facing = 1 - 2 * (cols // 2)
    here_facing = 1 - 2 * here_core
    far_x = ((bucket // 8 - here_x) * facing) % 4
    far_z = ((bucket % 8 - here_z) * facing) % 8
    blk = jnp.where(cols % 2 == 0, far_z * 4 + far_x, 32 + far_x * 8 + far_z)
    block_ids = jnp.arange(BLOCKS, dtype=jnp.int32)
    target = jnp.sum(
        jnp.where(tile_rows[0, 0][:, None] == block_ids[None, :], row_slot[0][None, :], 0), axis=1
    )
    ahead = ((target // 8 - here_x) * here_facing) % 4
    chunk = jnp.where(ahead == 3, 1, jnp.where(ahead == 0, 0, ahead + 1))
    row = chunk * 8 + ((target % 8 - here_z) * here_facing) % 8

    with jax.named_scope("gather"):
        mine = lax.dynamic_slice_in_dim(sketch, here_core * 2 * EDGE, 2 * EDGE, 0)
        slab = join(ring_gather(mine[:EDGE], "x"))
        line = join(ring_gather(mine[EDGE:], "z"))
        first = ring_gather(slab, "z")
        second = ring_gather(line, "x")
        slab, *plan, counts = lax.optimization_barrier((slab, *slot_plan(bucket_fill[0, 0], side)))
        first[0] = slab
        early, final = [], []
        base = 0
        for found in (first, second):
            for distance, piece in enumerate(found):
                (final if distance == len(found) // 2 else early).append((base, piece))
                base += piece.shape[0]
        panels = place(final, base, place(early, base))
        panels_other = swap(panels)

    stack = tiles[0, 0]
    tables = [(counts, listed, blk, row) for listed in plan]
    (sums,) = slot_products(0, tables[0], stack, panels)
    own, behind, ahead, far = slot_products(1, tables[1], stack, panels_other, sums)

    with jax.named_scope("scatter_rows"):
        passing = shift(far, "x", 1)
        from_ahead = shift(behind, "x", -1)
        own = own + from_ahead + shift(ahead + passing, "x", 1)
        passing = shift(own[4], "z", 1)
        ahead = jnp.stack([own[2], own[3] + passing])
        ahead, behind = lax.optimization_barrier((ahead, own[5:7]))
        ahead, behind = shift(ahead, "z", 2), shift(behind, "z", -2)
        middle = own[0] + ahead[0] + behind[1]
        ahead, behind = lax.optimization_barrier((own[1] + ahead[1], own[7] + behind[0]))
        product_rows = middle + shift(ahead, "z", 1) + shift(behind, "z", -1)

    with jax.named_scope("gram"):
        gram = jnp.dot(
            product_rows.T,
            product_rows,
            precision=lax.Precision.HIGHEST,
            preferred_element_type=jnp.float32,
        )
        ring = ("y", "core", "x")
        part = jnp.sum(exchange(gram, ring).reshape(32, 8, WIDTH), axis=0)
        part = jnp.sum(
            exchange(jnp.broadcast_to(part[None], (8, 8, WIDTH)), "z"), axis=0
        )
        gram = exchange(jnp.broadcast_to(part[None], (32, 8, WIDTH)), ring).reshape(WIDTH, WIDTH)

    embedding, factor = factor_and_solve(gram, product_rows)
    return embedding, factor


def solution(mesh):
    fine = Mesh(mesh.devices.reshape(SIZES), AXES)
    grp, col = ("y", "core"), ("x", "z")
    placed = (
        P(grp, col, None, None, None),
        P(grp, col, None),
        P(grp, col, None),
        P(grp, col, None),
        P(grp, None),
        P(col, None),
    )
    return jax.shard_map(
        on_device,
        mesh=fine,
        in_specs=placed,
        out_specs=(P(AXES, None), P()),
        check_vma=False,
    )
```

```python
import functools

import jax
import jax.numpy as jnp
from jax import lax
from jax.experimental import pallas as pl
from jax.experimental.pallas import tpu as pltpu
from jax.sharding import Mesh
from jax.sharding import PartitionSpec as P

AXES = ("y", "core", "x", "z")
SIZES = (4, 2, 4, 8)
EDGE = 128
WIDTH = 256
BLOCKS = 32
BUCKETS = 32
PER_BUCKET = 6
SLOTS = 192
ROWS = 32768
GROUP = 8
HELD = 96
LIMIT = 30
FAR_ROW = 24


def shift(value, axis, step):
    count = lax.axis_size(axis)
    pairs = [
        (core * count + i, core * count + (i + step - 2 * core * step) % count)
        for core in range(2)
        for i in range(count)
    ]
    return lax.ppermute(value, ("core", axis), pairs)


def swap(value):
    return lax.ppermute(value, "core", [(0, 1), (1, 0)])


def ring_gather(block, axis):
    count = lax.axis_size(axis)
    found = [None] * count
    found[0] = behind = ahead = block
    for step in range(1, count // 2):
        behind = shift(behind, axis, 1)
        ahead = shift(ahead, axis, -1)
        found[count - step] = behind
        found[step] = ahead
    behind, ahead = lax.optimization_barrier((behind, ahead))
    found[count // 2 + 1], found[count // 2 - 1] = behind, ahead
    found[count // 2] = shift(behind, axis, 1)
    return found


def join_kernel(*refs):
    out = refs[-1]
    offset = 0
    for piece in refs[:-1]:
        length = piece.shape[0]
        out[pl.ds(offset, length), :] = piece[...]
        offset += length


def join(pieces):
    total = sum(piece.shape[0] for piece in pieces)
    vmem = pl.BlockSpec(memory_space=pltpu.VMEM)
    return pl.pallas_call(
        join_kernel,
        out_shape=jax.ShapeDtypeStruct((total, WIDTH), jnp.float32),
        in_specs=[vmem] * len(pieces),
        out_specs=vmem,
        compiler_params=pltpu.CompilerParams(vmem_limit_bytes=8 * 1024 * 1024),
        cost_estimate=pl.CostEstimate(flops=0, bytes_accessed=total * WIDTH * 8, transcendentals=0),
        name="join",
    )(*pieces)


def place_kernel(offsets, late, *refs):
    pieces, out, sem = refs[late:-2], refs[-2], refs[-1]
    copies = [
        pltpu.make_async_copy(piece, out.at[pl.ds(offset, piece.shape[0])], sem.at[n])
        for n, (piece, offset) in enumerate(zip(pieces, offsets))
    ]
    for copy in copies:
        copy.start()
    for copy in copies:
        copy.wait()


def place(pieces, total, before=None):
    late = before is not None
    vmem = pl.BlockSpec(memory_space=pltpu.VMEM)
    any_space = pl.BlockSpec(memory_space=pl.ANY)
    offsets, arrays = zip(*pieces)
    moved = sum(array.size for array in arrays) * 8
    return pl.pallas_call(
        functools.partial(place_kernel, offsets, int(late)),
        out_shape=jax.ShapeDtypeStruct((total, WIDTH), jnp.float32),
        in_specs=[any_space] * late + [vmem] * len(arrays),
        out_specs=any_space,
        input_output_aliases={0: 0} if late else {},
        scratch_shapes=[pltpu.SemaphoreType.DMA((len(arrays),))],
        compiler_params=pltpu.CompilerParams(vmem_limit_bytes=16 * 1024 * 1024),
        cost_estimate=pl.CostEstimate(flops=0, bytes_accessed=moved, transcendentals=0),
        name="place",
    )(*([before] if late else []), *arrays)


def plan_kernel(fill, kind, *refs):
    plan, counts = refs[:3], refs[3]

    def list_bucket(b, ends):
        def put(j, ends):
            slot = b * PER_BUCKET + j
            which = kind[slot]
            for k in range(3):
                plan[k][ends[k]] = slot
            return tuple(e + (which == k).astype(jnp.int32) for k, e in enumerate(ends))

        return lax.fori_loop(0, fill[b], put, ends)

    ends = lax.fori_loop(0, BUCKETS, list_bucket, (0, 0, 0))
    for k in range(3):
        counts[k] = ends[k]


def slot_plan(fill, kind):
    smem = pl.BlockSpec(memory_space=pltpu.SMEM)
    return pl.pallas_call(
        plan_kernel,
        out_shape=[jax.ShapeDtypeStruct((SLOTS,), jnp.int32)] * 3
        + [jax.ShapeDtypeStruct((3,), jnp.int32)],
        in_specs=[smem, smem],
        out_specs=[smem] * 4,
        compiler_params=pltpu.CompilerParams(vmem_limit_bytes=1024 * 1024),
        cost_estimate=pl.CostEstimate(flops=0, bytes_accessed=12 * 1024 * 1024, transcendentals=0),
        name="slot_plan",
    )(fill, kind)


def products_kernel(part, counts, listed, blk, row, tiles, panels, *refs):
    first_row = FAR_ROW if part == 1 else 0
    if part == 0:
        total, held, tile_sem = refs
    else:
        before, outs = refs[0], refs[1:-3]
        total, held, tile_sem = refs[-3:]
    count = counts[part]

    def tile_copy(i):
        spot = lax.rem(i, HELD)
        return pltpu.make_async_copy(tiles.at[listed[i]], held.at[spot], tile_sem.at[spot])

    def fetch(load):
        @pl.loop(load * HELD, jnp.minimum((load + 1) * HELD, count))
        def _(i):
            tile_copy(i).start()

    fetch(0)
    total[...] = before[first_row : first_row + total.shape[0]] if part else jnp.zeros_like(total)

    def product(i):
        slot = listed[i]
        tile = held[lax.rem(i, HELD)]
        panel = panels[pl.ds(pl.multiple_of(blk[slot] * EDGE, EDGE), EDGE), :]
        tile_hi = tile.astype(jnp.bfloat16)
        tile_lo = (tile - tile_hi.astype(jnp.float32)).astype(jnp.bfloat16)
        panel_hi = panel.astype(jnp.bfloat16)
        panel_lo = (panel - panel_hi.astype(jnp.float32)).astype(jnp.bfloat16)
        left = jnp.concatenate([tile_hi, tile_hi, tile_lo], axis=1)
        right = jnp.concatenate([panel_hi, panel_lo, panel_hi], axis=0)
        return jnp.dot(left, right, preferred_element_type=jnp.float32)

    @pl.loop(0, pl.cdiv(count, HELD))
    def _(load):
        first = load * HELD
        last = jnp.minimum(first + HELD, count)
        groups = (last - first) // GROUP

        @pl.loop(0, groups)
        def _(g):
            slots = [first + g * GROUP + n for n in range(GROUP)]
            for i in slots:
                tile_copy(i).wait()
            sums = [product(i) for i in slots]
            for i, value in zip(slots, sums):
                total[row[listed[i]] - first_row] += value

        @pl.loop(first + groups * GROUP, last)
        def _(i):
            tile_copy(i).wait()
            total[row[listed[i]] - first_row] += product(i)

        fetch(load + 1)

    if part:
        offset = 0
        for out in outs:
            length = out.shape[0]
            out[...] = total[offset : offset + length]
            offset += length


def slot_products(part, tables, tiles, panels, before=None):
    any_space = pl.BlockSpec(memory_space=pl.ANY)
    smem = pl.BlockSpec(memory_space=pltpu.SMEM)
    vmem = pl.BlockSpec(memory_space=pltpu.VMEM)
    block = lambda n: jax.ShapeDtypeStruct((n, EDGE, WIDTH), jnp.float32)
    scratch = [pltpu.VMEM((HELD, EDGE, EDGE), jnp.float32), pltpu.SemaphoreType.DMA((HELD,))]
    arrays = [tiles, panels]
    if part == 0:
        shapes = [block(BLOCKS)]
    else:
        shapes = [block(8)] if part == 1 else [block(8)] * 3
        rows = BLOCKS - FAR_ROW if part == 1 else FAR_ROW
        scratch = [pltpu.VMEM((rows, EDGE, WIDTH), jnp.float32)] + scratch
        arrays.append(before)
    share = (4, 1, 3)[part]
    return pl.pallas_call(
        functools.partial(products_kernel, part),
        out_shape=shapes,
        in_specs=[smem] * 4 + [any_space] + [vmem] * (len(arrays) - 1),
        out_specs=[vmem] * len(shapes),
        scratch_shapes=scratch,
        compiler_params=pltpu.CompilerParams(vmem_limit_bytes=LIMIT * 1024 * 1024),
        cost_estimate=pl.CostEstimate(
            flops=share * SLOTS * EDGE * EDGE * WIDTH,
            bytes_accessed=share * 3 * 1024 * 1024,
            transcendentals=0,
        ),
        name="slot_products",
    )(*tables, *arrays)


BAND = 64


def factor_kernel(gram, rows, embedding, factor, work):
    work[:, :WIDTH] = gram[...]
    work[:, WIDTH:] = rows[...].T
    lane = lax.broadcasted_iota(jnp.int32, (8, EDGE), 1)
    sub = lax.broadcasted_iota(jnp.int32, (8, EDGE), 0)
    columns = (WIDTH + EDGE) // EDGE

    def along_lanes(value, at):
        return jnp.broadcast_to(value[:, at : at + 1], (8, EDGE))

    def along_rows(value, at):
        return jnp.broadcast_to(value[at : at + 1, :], (8, EDGE))

    for band in range(WIDTH // BAND):
        top = band * BAND
        lead = top // EDGE
        strips = BAND // 8
        held = [
            [work[top + 8 * s : top + 8 * s + 8, c * EDGE : (c + 1) * EDGE] for c in range(lead, columns)]
            for s in range(strips)
        ]
        for s0 in range(strips):
            at = (top + 8 * s0) % EDGE
            cols = {s: [along_lanes(held[s][0], at + q) for q in range(8)] for s in range(s0, strips)}
            block = {(t, r): along_rows(cols[s0][r], t) for t in range(8) for r in range(t + 1)}
            lower = {}
            inverse = []
            root = []
            for q in range(8):
                inverse.append(1.0 / block[q, q])
                root.append(lax.rsqrt(block[q, q]))
                for t in range(q + 1, 8):
                    lower[t, q] = block[t, q] * inverse[q]
                for t in range(q + 1, 8):
                    for r in range(q + 1, t + 1):
                        block[t, r] = block[t, r] - lower[t, q] * block[r, q]
            lines = []
            for q in range(8):
                line = [along_rows(v, q) for v in held[s0]]
                for t in range(q):
                    line = [v - lower[q, t] * w for v, w in zip(line, lines[t])]
                lines.append(line)
            for s in range(s0 + 1, strips):
                weights = []
                for q in range(8):
                    value = cols[s][q]
                    for t in range(q):
                        value = value - lower[q, t] * weights[t]
                    weights.append(value)
                weights = [v * w for v, w in zip(weights, inverse)]
                for c in range(len(held[s])):
                    terms = [weights[q] * lines[q][c] for q in range(8)]
                    while len(terms) > 1:
                        terms = [a + b for a, b in zip(terms[::2], terms[1::2])]
                    held[s][c] = held[s][c] - terms[0]
            final = [jnp.zeros((8, EDGE), jnp.float32)] * len(held[s0])
            for q in range(8):
                final = [jnp.where(sub == q, w * root[q], v) for v, w in zip(final, lines[q])]
            for c in range(lead, columns):
                value = final[c - lead]
                if c < WIDTH // EDGE:
                    value = jnp.where(lane + c * EDGE >= sub + (top + 8 * s0), value, 0.0)
                work[top + 8 * s0 : top + 8 * s0 + 8, c * EDGE : (c + 1) * EDGE] = value
        below = top + BAND
        if below < WIDTH:
            base = below // EDGE * EDGE
            left = work[top:below, base:WIDTH]
            right = work[top:below, base:]
            update = lax.dot_general(
                left,
                right,
                (((0,), (0,)), ((), ())),
                precision=lax.Precision.HIGHEST,
                preferred_element_type=jnp.float32,
            )
            work[below:, base:] -= update[below - base :, :]
    scale = jnp.sqrt(jnp.float32(ROWS))
    for band in range(WIDTH // BAND):
        top = band * BAND
        lead = top // EDGE * EDGE
        if lead:
            factor[top : top + BAND, :lead] = jnp.zeros((BAND, lead), jnp.float32)
        factor[top : top + BAND, lead:] = work[top : top + BAND, lead:WIDTH] / scale
    embedding[...] = work[:, WIDTH:].T * scale


def factor_and_solve(gram, rows):
    vmem = pl.BlockSpec(memory_space=pltpu.VMEM)
    return pl.pallas_call(
        factor_kernel,
        out_shape=[
            jax.ShapeDtypeStruct((EDGE, WIDTH), jnp.float32),
            jax.ShapeDtypeStruct((WIDTH, WIDTH), jnp.float32),
        ],
        in_specs=[vmem, vmem],
        out_specs=[vmem, vmem],
        scratch_shapes=[pltpu.VMEM((WIDTH, WIDTH + EDGE), jnp.float32)],
        compiler_params=pltpu.CompilerParams(vmem_limit_bytes=16 * 1024 * 1024),
        name="factor_and_solve",
    )(gram, rows)


def exchange(value, axes):
    return lax.all_to_all(value, axes, 0, 0, tiled=True)


def on_device(tiles, tile_rows, tile_cols, bucket_fill, row_slot, sketch):
    here_x = lax.axis_index("x")
    here_z = lax.axis_index("z")
    here_core = lax.axis_index("core")

    slot_ids = jnp.arange(SLOTS, dtype=jnp.int32)
    bucket = slot_ids // PER_BUCKET
    cols = tile_cols[0, 0]
    side = (cols // 2 + here_core) % 2
    facing = 1 - 2 * (cols // 2)
    here_facing = 1 - 2 * here_core
    far_x = ((bucket // 8 - here_x) * facing) % 4
    far_z = ((bucket % 8 - here_z) * facing) % 8
    blk = jnp.where(cols % 2 == 0, far_z * 4 + far_x, 32 + far_x * 8 + far_z)
    block_ids = jnp.arange(BLOCKS, dtype=jnp.int32)
    target = jnp.sum(
        jnp.where(tile_rows[0, 0][:, None] == block_ids[None, :], row_slot[0][None, :], 0), axis=1
    )
    ahead = ((target // 8 - here_x) * here_facing) % 4
    chunk = jnp.where(ahead == 3, 1, jnp.where(ahead == 0, 0, ahead + 1))
    row = chunk * 8 + ((target % 8 - here_z) * here_facing) % 8
    kind = jnp.where(side == 0, 0, jnp.where(row >= FAR_ROW, 1, 2))

    with jax.named_scope("gather"):
        mine = lax.dynamic_slice_in_dim(sketch, here_core * 2 * EDGE, 2 * EDGE, 0)
        slab = join(ring_gather(mine[:EDGE], "x"))
        line = join(ring_gather(mine[EDGE:], "z"))
        first = ring_gather(slab, "z")
        second = ring_gather(line, "x")
        slab, *plan, counts = lax.optimization_barrier((slab, *slot_plan(bucket_fill[0, 0], kind)))
        first[0] = slab
        early, final = [], []
        base = 0
        for found in (first, second):
            for distance, piece in enumerate(found):
                (final if distance == len(found) // 2 else early).append((base, piece))
                base += piece.shape[0]
        panels = place(final, base, place(early, base))
        panels_other = swap(panels)

    stack = tiles[0, 0]
    tables = [(counts, listed, blk, row) for listed in plan]
    (sums,) = slot_products(0, tables[0], stack, panels)
    (far,) = slot_products(1, tables[1], stack, panels_other, sums)
    own, behind, ahead = slot_products(2, tables[2], stack, panels_other, sums)

    with jax.named_scope("scatter_rows"):
        passing = shift(far, "x", 1)
        from_ahead = shift(behind, "x", -1)
        own = own + from_ahead + shift(ahead + passing, "x", 1)
        passing = shift(own[4], "z", 1)
        ahead = jnp.stack([own[2], own[3] + passing])
        ahead, behind = lax.optimization_barrier((ahead, own[5:7]))
        ahead, behind = shift(ahead, "z", 2), shift(behind, "z", -2)
        middle = own[0] + ahead[0] + behind[1]
        ahead, behind = lax.optimization_barrier((own[1] + ahead[1], own[7] + behind[0]))
        product_rows = middle + shift(ahead, "z", 1) + shift(behind, "z", -1)

    with jax.named_scope("gram"):
        gram = jnp.dot(
            product_rows.T,
            product_rows,
            precision=lax.Precision.HIGHEST,
            preferred_element_type=jnp.float32,
        )
        ring = ("y", "core", "x")
        part = jnp.sum(exchange(gram, ring).reshape(32, 8, WIDTH), axis=0)
        part = jnp.sum(
            exchange(jnp.broadcast_to(part[None], (8, 8, WIDTH)), "z"), axis=0
        )
        gram = exchange(jnp.broadcast_to(part[None], (32, 8, WIDTH)), ring).reshape(WIDTH, WIDTH)

    embedding, factor = factor_and_solve(gram, product_rows)
    return embedding, factor


def solution(mesh):
    fine = Mesh(mesh.devices.reshape(SIZES), AXES)
    grp, col = ("y", "core"), ("x", "z")
    placed = (
        P(grp, col, None, None, None),
        P(grp, col, None),
        P(grp, col, None),
        P(grp, col, None),
        P(grp, None),
        P(col, None),
    )
    return jax.shard_map(
        on_device,
        mesh=fine,
        in_specs=placed,
        out_specs=(P(AXES, None), P()),
        check_vma=False,
    )
```
